256 devices in a mesh: group: 2 (over core), expert: 32 (over y, z), mp: 4 (over x).
Axes of the slice: x: 4, y: 4, z: 8, core: 2. Of those that a mesh axis runs over, the one named last changes fastest.
Arguments:
- rows: bfloat16 [2, 2048, 2048], P('group', 'expert'), may hold values from -6 to 6
- route: int32 [2, 2048, 2], P('group', 'expert'), may hold values from 0 to 31, all different within a row; in each aligned block of 64 rows (0 to 63, 64 to 127, ..., all dimensions but the last counted through in order) at most 8 rows name the same one
- gate_int: int32 [2, 2048, 2], P('group', 'expert'), may hold values from 1 to 31
- moe_gain: float32 [2, 2048], P('group'), may hold values from 0.1 to 1.9
- w_in: bfloat16 [2, 32, 2048, 4096], P('group', 'expert', None, 'mp'), may hold values from -0.125 to 0.125
- w_out: bfloat16 [2, 32, 4096, 2048], P('group', 'expert', 'mp'), may hold values from -0.09375 to 0.09375
- attn_gain: float32 [2, 2048], P('group'), may hold values from 0.1 to 1.9
- attn_weight: bfloat16 [2, 2048, 2, 1024], P('group', None, None, 'mp'), may hold values from -0.125 to 0.125
- src_len: int32 [32, 6], P('expert'), may hold values from 1 to 16, 64 in all within a row
- target: int32 [32, 6], P('expert'), may hold values from 0 to 2047, as said below
- cache: bfloat16 [2048, 16, 2, 1024], P('expert', None, None, 'mp'), may hold values from -128 to 128
- cache_len: int32 [2048], P('expert'), may hold values from 1 to 16
Outputs:
- moe_out: bfloat16 [2, 2048, 2048], P('group', 'expert')
- step_out: bfloat16 [2, 2048, 2048], P('group', 'expert')
The draws below stay inside these ranges and needn't reach their ends.
Inputs may be any that keep to these rules, and one draw needn't show every extreme that they name: `route`: the rows of one device name one expert at most 8 times. `src_len`: the 6 lengths of one row sum to 64. `target`: all targets are different slots.
All inputs are finite; a program needn't handle non-finite values.
Results may differ from the reference program's by a relative error of at most 0.035.
Values may be sent and summed in bfloat16 or wider, within the bound.
No kernel may reach another device: no remote copies, remote signals or barrier semaphores. Data moves between devices by JAX's collectives and lax.ppermute only.
A program may use at most 64 MiB of HBM per device.

```python
import math
import jax
import jax.numpy as jnp
import numpy as np
from jax import lax

D = 2048
HEADS = 8
HEAD_DIM = 128
FFW = 4096
ROWS = 64
SRC_DEV = 6
SRC_MAX = 16
EXPERTS = 32
CAPACITY = 8
TOKENS = 2048
N_EXPERT = 32


def draw_target(key, part):
    key = jax.random.fold_in(key, 11)
    offset_key, order_key = jax.random.split(key)
    count = N_EXPERT
    extra = jax.random.randint(offset_key, (SRC_DEV,), 0, count).astype(jnp.int32)
    fixed_offsets = jnp.array([0, 1, count - 1, count // 2], jnp.int32)
    column = jnp.arange(SRC_DEV, dtype=jnp.int32)
    padded = jnp.concatenate([fixed_offsets, jnp.zeros((SRC_DEV,), jnp.int32)])[:SRC_DEV]
    offsets = jnp.where(column < 4, padded, extra)
    order_keys = jax.random.split(order_key, count)
    orders = jax.vmap(lambda one: jax.random.permutation(one, ROWS))(order_keys).astype(jnp.int32)
    encoder_index = jnp.arange(count, dtype=jnp.int32)[:, None]
    destination = (encoder_index + offsets[None, :]) % count
    local = orders[destination, column[None, :]]
    return (destination * ROWS + local).astype(jnp.int32)


def draw_cache(key, part):
    key = jax.random.fold_in(key, 23)
    shape = (ROWS * N_EXPERT, SRC_MAX, 2, HEADS * HEAD_DIM)
    first_key = jax.random.fold_in(key, 0)
    values = jnp.clip(jax.random.normal(first_key, shape, jnp.float32), -6.0, 6.0)
    return values.astype(jnp.bfloat16)


def touch_ends(values, own_key, least, largest):
    longest = values.shape.index(max(values.shape))
    spots = []
    for shift in (0, 1):
        where = [jax.random.randint(jax.random.fold_in(own_key, axis), (), 0, length) for axis, length in enumerate(values.shape)]
        where[longest] = (where[longest] + shift) % values.shape[longest]
        spots.append(tuple(where))
    return values.at[spots[0]].set(least).at[spots[1]].set(largest)


def shard_levels(own_key, dims, cuts, smallest, top_value):
    def one(axis_at, parts):
        steps = jax.random.uniform(jax.random.fold_in(jax.random.fold_in(own_key, 6), axis_at), (parts,), jnp.float32, smallest / len(cuts), top_value / len(cuts))
        return jnp.repeat(jnp.exp(steps), dims[axis_at] // parts).reshape((-1,) + (1,) * (len(dims) - axis_at - 1))

    factor_of = one(*cuts[0])
    for cut in cuts[1:]:
        factor_of = factor_of * one(*cut)
    return factor_of


def length_profile(amount, total, limit, slope):
    weights = [(1 << 20) // math.isqrt(grade ** slope) + 1 for grade in range(2, amount + 1)]
    spare, holding = total - limit - (amount - 1), [1] * (amount - 1)
    while spare > 0:
        movable = [i for i in range(amount - 1) if holding[i] < limit]
        whole, budget = sum([weights[i] for i in movable]), spare
        for i in movable:
            more = min(limit - holding[i], max(1, budget * weights[i] // whole), spare)
            holding[i] = holding[i] + more
            spare = spare - more
    return np.array([limit] + holding)


def uneven(own_key, count, total, limit, skew):
    if count == 2:
        one = jax.random.randint(own_key, (), max(1, total - limit), min(limit, total - 1) + 1)
        return jnp.stack([one, total - one])
    tallies = jnp.asarray(length_profile(count, total, limit, skew), jnp.int32)
    couples = (count - 1) // 2
    source_of, sink = tallies[1:1 + 2 * couples:2], tallies[2:2 + 2 * couples:2]
    room = jnp.minimum(source_of - 1, limit - sink)
    passed = jax.random.randint(jax.random.fold_in(own_key, 1), (couples,), 0, 1 << 20) % (room + 1)
    tallies = tallies.at[1:1 + 2 * couples:2].set(source_of - passed).at[2:2 + 2 * couples:2].set(sink + passed)
    return tallies[jax.random.permutation(jax.random.fold_in(own_key, 2), count)]


def deal_out(stream_key, own, number, rows, amount, top, most, slope):
    order = jax.random.permutation(stream_key, amount)
    crowded, ordinary = load_shares(amount, rows * top, most, slope, True), load_shares(amount, rows * top, most, slope, False)
    places = jnp.arange(amount)

    def named(sizes, turn):
        used = int((sizes > 0).sum())
        fixed = max(1, used // 4)
        passed = fixed + (places - fixed + turn * (used - fixed)) % max(1, amount - fixed)
        return jnp.zeros((amount,), jnp.int32).at[order[jnp.where(places < fixed, places, passed)]].set(jnp.asarray(sizes, jnp.int32))

    sizes = jnp.where(number % 4 == 0, named(crowded, number // 4), named(ordinary, number - number // 4 - 1))
    mixed = jax.random.permutation(jax.random.fold_in(own, 3), amount)
    donor, sink = mixed[0:amount // 2 * 2:2], mixed[1:amount // 2 * 2:2]
    room = jnp.minimum(sizes[donor] - 1, most - sizes[sink]) // 2
    room = jnp.where((donor == order[0]) | (sink == order[0]) | (sizes[sink] == 0), 0, jnp.maximum(room, 0))
    passed = jax.random.randint(jax.random.fold_in(own, 4), (amount // 2,), 0, 1 << 20) % (room + 1)
    sizes = sizes.at[donor].add(-passed).at[sink].add(passed)
    members = jnp.searchsorted(jnp.cumsum(sizes), jnp.arange(rows * top), side="right").astype(jnp.int32)
    listing = members.reshape(top, rows).T
    listing = listing[jax.random.permutation(jax.random.fold_in(own, 1), rows)]
    turn = jax.random.randint(jax.random.fold_in(own, 2), (rows, 1), 0, top)
    return jnp.take_along_axis(listing, (jnp.arange(top)[None, :] + turn) % top, axis=1)


def load_shares(number_of, total, reach, lean, full):
    weights = [(1 << 20) // math.isqrt(grade ** lean) + 1 for grade in range(1, number_of + 1)]
    largest = reach if full else min(reach, max(-(-total // number_of), total * weights[0] // sum(weights)))
    least = 1 if total - largest >= number_of - 1 else 0
    counts, spare = [largest] + [least] * (number_of - 1), total - largest - least * (number_of - 1)
    while spare > 0:
        movable = [i for i in range(1, number_of) if counts[i] < largest] or [i for i in range(1, number_of) if counts[i] < reach]
        mass, remaining = sum([weights[i] for i in movable]), spare
        for i in movable:
            addition = min(reach - counts[i], max(1, remaining * weights[i] // mass), spare)
            counts[i] = counts[i] + addition
            spare = spare - addition
    return np.array(counts)


def bell_draw(rng, dims, scale, limit, shards=(), kind=jnp.bfloat16):
    entries = jax.random.normal(rng, dims, jnp.float32) * scale
    if len(shards) > 0:
        entries = shard_levels(rng, dims, shards, -0.22, 0.18) * entries
    return jnp.clip(entries, min=-limit, max=limit).astype(kind)


def setup_inputs(seed: int = 0) -> dict:
    key_of = jax.random.split(jax.random.key(seed), 13)
    rows = bell_draw(key_of[0], (2, TOKENS, D), 1.0, 6.0, ((0, 2), (1, 32)))
    route_keys = jax.random.split(jax.random.fold_in(key_of[1], 1), 2 * TOKENS // ROWS)
    route_turns = jax.random.permutation(jax.random.fold_in(key_of[1], 3), 2 * TOKENS // ROWS)
    route = jax.vmap(lambda own, number: deal_out(jax.random.fold_in(key_of[1], 2), own, number, ROWS, EXPERTS, 2, CAPACITY, 2))(route_keys, route_turns).reshape((2, TOKENS, 2))
    gate_int = touch_ends(jax.random.randint(key_of[2], (2, TOKENS, 2), 1, 32), jax.random.fold_in(key_of[2], 1), 1, 31).astype(jnp.int32)
    moe_gain = jnp.clip(1.0 + 0.18 * jax.random.normal(key_of[3], (2, D), jnp.float32), 0.1, 1.9)
    w_in = bell_draw(key_of[4], (2, EXPERTS, D, FFW), D ** -0.5, 0.125, ((0, 2), (1, 32), (3, 4)))
    w_out = bell_draw(key_of[5], (2, EXPERTS, FFW, D), FFW ** -0.5, 0.09375, ((0, 2), (1, 32), (2, 4)))
    attn_gain = jnp.clip(1.0 + 0.18 * jax.random.normal(key_of[6], (2, D), jnp.float32), 0.1, 1.9)
    attn_weight = bell_draw(key_of[7], (2, D, 2, HEADS * HEAD_DIM), D ** -0.5, 0.125, ((0, 2), (3, 4)))
    src_len = jax.vmap(lambda own: uneven(own, SRC_DEV, ROWS, SRC_MAX, 2))(jax.random.split(key_of[8], N_EXPERT)).reshape((N_EXPERT, SRC_DEV)).astype(jnp.int32)
    target = draw_target(jax.random.fold_in(key_of[12], 71), 0)
    cache = draw_cache(jax.random.fold_in(key_of[12], 71), 0)
    cache_len = touch_ends(jax.random.randint(key_of[11], (TOKENS,), 1, SRC_MAX + 1), jax.random.fold_in(key_of[11], 1), 1, SRC_MAX).astype(jnp.int32)
    return dict(rows=rows, route=route, gate_int=gate_int, moe_gain=moe_gain, w_in=w_in, w_out=w_out, attn_gain=attn_gain, attn_weight=attn_weight, src_len=src_len, target=target, cache=cache, cache_len=cache_len)


def layer_norm(values, gain):
    center = values - lax.optimization_barrier(jnp.mean(values, axis=-1, keepdims=True))
    spread = lax.optimization_barrier(jnp.mean(center * center, axis=-1, keepdims=True))
    return center * lax.rsqrt(spread + 1e-05) * gain

def expert_layer(block, routes, gates, gain, first, second):
    base = block.astype(jnp.float32)
    normed = layer_norm(base, gain).astype(jnp.bfloat16)
    weights = gates.astype(jnp.float32)
    weights = weights / lax.optimization_barrier(jnp.sum(weights, axis=1, keepdims=True))
    room = N_EXPERT * CAPACITY

    def one_expert(total, which):
        hit = routes == which
        picked = lax.optimization_barrier(jnp.sum(jnp.where(hit, weights, 0.0), axis=1))
        used = jnp.any(hit, axis=1)
        index = jnp.nonzero(used, size=room, fill_value=0)[0].astype(jnp.int32)
        valid = jnp.arange(room) < jnp.sum(used.astype(jnp.int32))
        hidden = jax.nn.relu(jnp.dot(normed[index], first[which], preferred_element_type=jnp.float32)).astype(jnp.bfloat16)
        result = jnp.dot(hidden, second[which], preferred_element_type=jnp.float32).astype(jnp.bfloat16).astype(jnp.float32)
        scale = jnp.where(valid, picked[index], 0.0)
        return (total.at[index].add(scale[:, None] * result), None)
    start = jnp.zeros(base.shape, jnp.float32)
    summed, _ = lax.scan(one_expert, start, jnp.arange(first.shape[0], dtype=jnp.int32))
    return (base + summed).astype(jnp.bfloat16)

def reference(rows, route, gate_int, moe_gain, w_in, w_out, attn_gain, attn_weight, src_len, target, cache, cache_len):
    encoder_rows = expert_layer(rows[0], route[0], gate_int[0], moe_gain[0], w_in[0], w_out[0])
    decoder_rows = expert_layer(rows[1], route[1], gate_int[1], moe_gain[1], w_in[1], w_out[1])
    width = HEADS * HEAD_DIM
    encoded = layer_norm(encoder_rows.astype(jnp.float32), attn_gain[0]).astype(jnp.bfloat16)
    new_kv = jnp.dot(encoded, attn_weight[0].reshape(D, 2 * width), preferred_element_type=jnp.float32)
    new_kv = new_kv.astype(jnp.bfloat16).reshape(TOKENS, 2, width)
    normed_dec = layer_norm(decoder_rows.astype(jnp.float32), attn_gain[1]).astype(jnp.bfloat16)
    query = jnp.dot(normed_dec, attn_weight[1][:, 0, :], preferred_element_type=jnp.float32).astype(jnp.bfloat16)
    ends = jnp.cumsum(src_len, axis=1)
    starts = ends - src_len + (jnp.arange(N_EXPERT, dtype=jnp.int32) * ROWS)[:, None]
    starts = starts.reshape(-1).astype(jnp.int32)
    lengths = src_len.reshape(-1).astype(jnp.int32)
    owner = jnp.full((TOKENS,), -1, jnp.int32).at[target.reshape(-1)].set(jnp.arange(N_EXPERT * SRC_DEV, dtype=jnp.int32))
    freed = owner >= 0
    own = jnp.maximum(owner, 0)
    source_rows = starts[own][:, None] + jnp.arange(SRC_MAX, dtype=jnp.int32)[None, :]
    source_rows = jnp.clip(source_rows, 0, TOKENS - 1).astype(jnp.int32)
    slot_kv = jnp.where(freed[:, None, None, None], new_kv[source_rows], cache)
    slot_len = jnp.where(freed, lengths[own], cache_len)
    keys = slot_kv[:, :, 0, :].reshape(TOKENS, SRC_MAX, HEADS, HEAD_DIM).astype(jnp.float32)
    values = slot_kv[:, :, 1, :].reshape(TOKENS, SRC_MAX, HEADS, HEAD_DIM).astype(jnp.float32)
    heads_query = query.reshape(TOKENS, HEADS, HEAD_DIM).astype(jnp.float32)
    scores = jnp.einsum('thd,tphd->thp', heads_query, keys) * (1.0 / math.sqrt(HEAD_DIM))
    inside = jnp.arange(SRC_MAX)[None, None, :] < slot_len[:, None, None]
    scores = jnp.where(inside, scores, -1e+30)
    highest = lax.optimization_barrier(jnp.max(scores, axis=-1, keepdims=True))
    raised = jnp.where(inside, jnp.exp(scores - highest), 0.0)
    probs = (raised / lax.optimization_barrier(jnp.sum(raised, axis=-1, keepdims=True))).astype(jnp.bfloat16)
    context = jnp.einsum('thp,tphd->thd', probs.astype(jnp.float32), values).astype(jnp.bfloat16).reshape(TOKENS, width)
    output_map = attn_weight[1][:, 1, :]
    mixed = jnp.dot(context, output_map.T, preferred_element_type=jnp.float32)
    decoded = (decoder_rows.astype(jnp.float32) + mixed).astype(jnp.bfloat16)
    return (jnp.stack([encoder_rows, decoder_rows]), jnp.stack([encoded, decoded]))
```

```python
import math

import jax
import jax.numpy as jnp
from jax import lax
from jax.sharding import PartitionSpec as P

HEAD_DIM = 128
BF = jnp.bfloat16
F32 = jnp.float32


def layer_norm(values, gain):
    center = values - jnp.mean(values, axis=-1, keepdims=True)
    spread = jnp.mean(center * center, axis=-1, keepdims=True)
    return center * lax.rsqrt(spread + 1e-05) * gain


def ring_gather(block, axis, count, pairs_of=None):
    got = [block]
    for step in range(1, count):
        got.append(lax.ppermute(block, axis, [(i, (i + step) % count) for i in range(count)]))
    return got


def body(
    rows,
    route,
    gate_int,
    moe_gain,
    w_in,
    w_out,
    attn_gain,
    attn_weight,
    src_len,
    target,
    cache,
    cache_len,
):
    experts = lax.axis_size("expert")
    parts = lax.axis_size("mp")
    row_count = rows.shape[1]
    width = rows.shape[2]
    piece = width // parts
    group_place = lax.axis_index("group")
    expert_place = lax.axis_index("expert")
    mp_place = lax.axis_index("mp")
    capacity = 8
    head_width = attn_weight.shape[3]
    heads_here = head_width // HEAD_DIM
    positions = cache.shape[1]
    sources = src_len.shape[1]

    padded = jnp.full((8, 128), -1, jnp.int32).at[0, :sources].set(target[0])
    all_targets = lax.all_gather(padded, "expert", axis=0, tiled=False)[:, 0, :8]

    own_map = attn_weight[0][:, 1, :]
    maps = ring_gather(own_map, "mp", parts)

    base = rows[0].astype(F32)
    normed = layer_norm(base, moe_gain[0]).astype(BF)
    weights = gate_int[0].astype(F32)
    weights = weights / jnp.sum(weights, axis=1, keepdims=True)
    flat_dest = route[0].reshape(-1)
    onehot = (flat_dest[:, None] == jnp.arange(experts)[None, :]).astype(jnp.int32)
    position = jnp.sum((jnp.cumsum(onehot, axis=0) - 1) * onehot, axis=1)
    pair_index = (flat_dest * capacity + position).reshape(row_count, 2)
    slot_iota = jnp.arange(experts * capacity, dtype=jnp.int32)
    slot_table = (
        (slot_iota[:, None] == pair_index[None, :, 0])
        | (slot_iota[:, None] == pair_index[None, :, 1])
    ).astype(BF)
    buffer = jnp.dot(slot_table, normed, preferred_element_type=F32).astype(BF)
    buffer = buffer.reshape(experts, capacity, width)
    arrived = lax.all_to_all(buffer, "expert", split_axis=0, concat_axis=0, tiled=True)
    hidden = jax.nn.relu(
        jnp.einsum("sci,if->scf", arrived, w_in[0, 0], preferred_element_type=F32)
    ).astype(BF)
    partial_rows = jnp.einsum("scf,fo->sco", hidden, w_out[0, 0], preferred_element_type=F32)
    partial_rows = partial_rows.astype(BF).reshape(experts, capacity, parts, piece)
    partial_rows = partial_rows.transpose(0, 2, 1, 3).reshape(experts * parts, capacity, piece)
    returned = lax.all_to_all(
        partial_rows, ("expert", "mp"), split_axis=0, concat_axis=0, tiled=True
    )
    returned = returned.reshape(experts * parts * capacity, piece)
    cell = jnp.arange(experts * parts * capacity, dtype=jnp.int32)
    cell_slot = (cell // (parts * capacity)) * capacity + cell % capacity
    wanted = jnp.concatenate([pair_index[:, 0], pair_index[:, 1]])
    pick = (wanted[:, None] == cell_slot[None, :]).astype(BF)
    picked = jnp.dot(pick, returned, preferred_element_type=F32).astype(BF).astype(F32)
    added = weights[:, 0:1] * picked[:row_count] + weights[:, 1:2] * picked[row_count:]
    base_piece = lax.dynamic_slice_in_dim(base, mp_place * piece, piece, axis=1)
    moe_piece = (base_piece + added).astype(BF)

    pieces = ring_gather(moe_piece, "mp", parts)
    moe_rows = jnp.zeros((row_count, width), BF)
    for step, one in enumerate(pieces):
        place = (mp_place - step) % parts
        moe_rows = lax.dynamic_update_slice_in_dim(moe_rows, one, place * piece, axis=1)

    encoded = layer_norm(moe_rows.astype(F32), attn_gain[0]).astype(BF)
    projected = jnp.dot(
        encoded, attn_weight[0].reshape(width, 2 * head_width), preferred_element_type=F32
    ).astype(BF)
    query = projected[:, :head_width]

    local = all_targets.reshape(-1) - expert_place * row_count
    slots = jnp.arange(row_count, dtype=jnp.int32)
    freed = local[:, None] == slots[None, :]
    asked = jnp.dot(freed.astype(BF), query, preferred_element_type=F32).astype(BF)
    asked = lax.all_to_all(
        asked.reshape(experts, 8, head_width), "expert", split_axis=0, concat_axis=0, tiled=True
    )
    asked = jnp.sum(asked.astype(F32), axis=0).astype(BF)
    new_kv = lax.ppermute(projected, "group", [(0, 1)])
    lengths = src_len[0]
    ends = jnp.cumsum(lengths)
    starts = ends - lengths
    row_iota = jnp.arange(row_count, dtype=jnp.int32)
    mine = (row_iota[None, :] >= starts[:, None]) & (row_iota[None, :] < ends[:, None])
    mine = jnp.concatenate([mine, jnp.ones((8 - sources, row_count), bool)])

    def attend(one_query, keys, values, allowed):
        outs = []
        for head in range(heads_here):
            span = slice(head * HEAD_DIM, (head + 1) * HEAD_DIM)
            scores = lax.dot_general(
                one_query[:, span],
                keys[:, span],
                (((1,), (1,)), ((), ())),
                preferred_element_type=F32,
            ) * (1.0 / math.sqrt(HEAD_DIM))
            scores = jnp.where(allowed, scores, -1e30)
            highest = jnp.max(scores, axis=-1, keepdims=True)
            raised = jnp.where(allowed, jnp.exp(scores - highest), 0.0)
            probs = (raised / jnp.sum(raised, axis=-1, keepdims=True)).astype(BF)
            outs.append(jnp.dot(probs, values[:, span], preferred_element_type=F32).astype(BF))
        return jnp.concatenate(outs, axis=1)

    new_context = attend(asked, new_kv[:, :head_width], new_kv[:, head_width:], mine)
    own_target = jnp.concatenate([target[0], jnp.full((8 - sources,), -1, jnp.int32)])
    goes = (own_target // row_count)[None, :] == jnp.arange(experts)[:, None]
    sent = jnp.where(goes[:, :, None], new_context[None], jnp.zeros((), BF))
    back = lax.all_to_all(sent, "expert", split_axis=0, concat_axis=0, tiled=True)

    flat_cache = cache.reshape(row_count * positions, 2 * head_width)
    cache_row = jnp.arange(row_count * positions, dtype=jnp.int32)
    own = (cache_row[None, :] // positions == slots[:, None]) & (
        cache_row[None, :] % positions < cache_len[:, None]
    )
    own_context = attend(query, flat_cache[:, :head_width], flat_cache[:, head_width:], own)
    fresh = jnp.dot(
        freed.astype(BF).T, back.reshape(experts * 8, head_width), preferred_element_type=F32
    ).astype(BF)
    context = jnp.where(jnp.any(freed, axis=0)[:, None], fresh, own_context)
    contexts = ring_gather(context, "mp", parts)
    mixed = sum(
        lax.dot_general(one, map_of, (((1,), (1,)), ((), ())), preferred_element_type=F32)
        for one, map_of in zip(contexts, maps)
    )
    decoded = (moe_rows.astype(F32) + mixed).astype(BF)
    step_rows = jnp.where(group_place == 0, encoded, decoded)
    return (moe_rows[None], step_rows[None])


def solution(mesh):
    return jax.shard_map(
        body,
        mesh=mesh,
        in_specs=(
            P("group", "expert", None),
            P("group", "expert", None),
            P("group", "expert", None),
            P("group", None),
            P("group", "expert", None, "mp"),
            P("group", "expert", "mp", None),
            P("group", None),
            P("group", None, None, "mp"),
            P("expert", None),
            P("expert", None),
            P("expert", None, None, "mp"),
            P("expert"),
        ),
        out_specs=(P("group", "expert", None), P("group", "expert", None)),
        check_vma=False,
    )
```

```python
import functools
import math

import jax
import jax.numpy as jnp
from jax import lax
from jax.experimental import pallas as pl
from jax.experimental.pallas import tpu as pltpu
from jax.sharding import PartitionSpec as P

HEAD_DIM = 128
CAPACITY = 8
SEATS = 8
BF = jnp.bfloat16
F32 = jnp.float32
I32 = jnp.int32
EPS = 1e-05
SCALE = 1.0 / math.sqrt(HEAD_DIM)


def iota(shape, dim):
    return lax.broadcasted_iota(I32, shape, dim)


def dot(a, b):
    return jnp.dot(a, b, preferred_element_type=F32)


def dot_t(a, b):
    return lax.dot_general(a, b, (((1,), (1,)), ((), ())), preferred_element_type=F32)


def call(kernel, outs, scalars, arrays):
    smem = pl.BlockSpec(memory_space=pltpu.SMEM)
    vmem = pl.BlockSpec(memory_space=pltpu.VMEM)
    return pl.pallas_call(
        kernel,
        out_shape=outs,
        in_specs=[smem] * len(scalars) + [vmem] * len(arrays),
        out_specs=jax.tree.map(lambda _: vmem, outs),
        compiler_params=pltpu.CompilerParams(vmem_limit_bytes=40 * 2**20),
    )(*scalars, *arrays)


def to_column(row):
    n = row.shape[1]
    return jnp.sum(
        jnp.where(iota((n, n), 0) == iota((n, n), 1), row, jnp.zeros_like(row)),
        axis=1,
        keepdims=True,
    )


def stack_halves(value):
    half = value.shape[2] // 2
    return jnp.concatenate([value[:, :, :half], value[:, :, half:]], axis=1)


def dispatch_kernel(route_ref, rows_ref, gain_ref, out_ref, place_ref):
    experts = out_ref.shape[0]
    count, width = rows_ref.shape
    route = route_ref[...]
    first, second = route[0:1], route[1:2]
    names = iota((experts, count), 0)
    hit0 = names == first
    hit1 = names == second
    one0 = jnp.where(hit0, 1.0, 0.0)
    one1 = jnp.where(hit1, 1.0, 0.0)
    before = jnp.where(iota((count, count), 0) < iota((count, count), 1), 1.0, 0.0).astype(BF)
    seen0 = dot(one0.astype(BF), before)
    seen1 = dot(one1.astype(BF), before) + jnp.sum(one0, axis=1, keepdims=True)
    place0 = first * CAPACITY + jnp.sum(one0 * seen0, axis=0, keepdims=True).astype(I32)
    place1 = second * CAPACITY + jnp.sum(one1 * seen1, axis=0, keepdims=True).astype(I32)
    place_ref[0:1, :] = place0
    place_ref[1:2, :] = place1
    slots = iota((experts * CAPACITY, count), 0)
    table = jnp.where((slots == place0) | (slots == place1), 1.0, 0.0).astype(BF)
    values = rows_ref[...].astype(F32)
    center = values - jnp.mean(values, axis=-1, keepdims=True)
    spread = jnp.mean(center * center, axis=-1, keepdims=True)
    normed = (center * lax.rsqrt(spread + EPS) * gain_ref[...]).astype(BF)
    span = out_ref.shape[2]
    for pair in range(width // (2 * span)):
        both = [
            dot(table, normed[:, (2 * pair + i) * span : (2 * pair + i + 1) * span]).reshape(
                experts, CAPACITY, span
            )
            for i in range(2)
        ]
        out_ref[:, pair * 16 : pair * 16 + 16, :] = jnp.concatenate(both, axis=1).astype(BF)


def expert_kernel(rows_ref, w_in_ref, w_out_ref, out_ref):
    sources, _, span = rows_ref.shape
    width = w_in_ref.shape[0]
    total = None
    for pair in range(width // (2 * span)):
        both = rows_ref[:, pair * 16 : pair * 16 + 16, :].astype(F32)
        for i in range(2):
            one = both[:, i * CAPACITY : (i + 1) * CAPACITY, :].reshape(sources * CAPACITY, span)
            at = (2 * pair + i) * span
            term = dot(one.astype(BF), w_in_ref[at : at + span, :])
            total = term if total is None else total + term
    hidden = jnp.maximum(total, 0.0).astype(BF)
    parts = out_ref.shape[1]
    piece = width // parts
    for part in range(parts):
        done = dot(hidden, w_out_ref[:, part * piece : (part + 1) * piece])
        out_ref[:, part] = stack_halves(done.reshape(sources, CAPACITY, piece)).astype(BF)


def combine_kernel(mp_ref, place_ref, gate_ref, rows_ref, back_ref, out_ref):
    parts = rows_ref.shape[1] // out_ref.shape[1]
    count, piece = out_ref.shape
    cells = back_ref.shape[0] * back_ref.shape[1]
    half = back_ref.shape[2]
    place = place_ref[...]
    gate = gate_ref[...].astype(F32)
    gate0 = to_column(gate[0:1])
    gate1 = to_column(gate[1:2])
    whole = gate0 + gate1
    cell = iota((count, cells), 1)
    cell_slot = (cell // (parts * 16)) * CAPACITY + cell % CAPACITY
    cell_half = (cell // CAPACITY) % 2
    keys = [jnp.where(cell_half == side, cell_slot, -1) for side in range(2)]
    picks = []
    for which in range(2):
        wanted = to_column(place[which : which + 1])
        for side in range(2):
            picks.append(jnp.where(keys[side] == wanted, 1.0, 0.0).astype(BF))
    got = dot(jnp.concatenate(picks, axis=0), back_ref[...].reshape(cells, half))
    got = got.astype(BF).astype(F32)
    row0 = jnp.concatenate([got[0:count], got[count : 2 * count]], axis=1)
    row1 = jnp.concatenate([got[2 * count : 3 * count], got[3 * count :]], axis=1)
    at = pl.multiple_of(mp_ref[0] * piece, piece)
    base = rows_ref[:, pl.ds(at, piece)].astype(F32)
    out_ref[...] = (base + ((gate0 / whole) * row0 + (gate1 / whole) * row1)).astype(BF)


def project_kernel(
    mp_ref, one_ref, two_ref, three_ref, four_ref, gain_ref, maps_ref, local_ref,
    moe_ref, encoded_ref, projected_ref, asked_ref,
):
    refs = [one_ref, two_ref, three_ref, four_ref]
    parts = len(refs)
    count, piece = one_ref.shape
    width = parts * piece
    blocks = [ref[...].astype(F32) for ref in refs]
    mean = sum(jnp.sum(block, axis=1, keepdims=True) for block in blocks) / width
    centers = [block - mean for block in blocks]
    spread = sum(jnp.sum(c * c, axis=1, keepdims=True) for c in centers) / width
    scale = lax.rsqrt(spread + EPS)
    total = None
    for step in range(parts):
        place = lax.rem(mp_ref[0] + (parts - step), parts)
        at = pl.ds(pl.multiple_of(place * piece, piece), piece)
        moe_ref[:, at] = refs[step][...]
        encoded = (centers[step] * scale * gain_ref[:, at]).astype(BF)
        encoded_ref[:, at] = encoded
        term = dot(encoded, maps_ref[at, :])
        total = term if total is None else total + term
    projected = total.astype(BF)
    projected_ref[...] = projected
    experts = asked_ref.shape[0]
    head_width = projected.shape[1] // 2
    query = projected[:, :head_width]
    wanted = to_column(local_ref[...])
    freed = jnp.where(iota((wanted.shape[0], count), 1) == wanted, 1.0, 0.0).astype(BF)
    asked = dot(freed, query).reshape(experts, SEATS, head_width)
    asked_ref[...] = stack_halves(asked).astype(BF)


def softmax(scores, allowed):
    scores = jnp.where(allowed, scores * SCALE, -1e30)
    raised = jnp.where(
        allowed, jnp.exp(scores - jnp.max(scores, axis=1, keepdims=True)), 0.0
    )
    return (raised / jnp.sum(raised, axis=1, keepdims=True)).astype(BF)


def source_kernel(length_ref, target_ref, asked_ref, fresh_ref, out_ref, *, slots):
    experts = asked_ref.shape[0]
    count = fresh_ref.shape[0]
    head_width = fresh_ref.shape[1] // 2
    asked = jnp.sum(asked_ref[...].astype(F32), axis=0).astype(BF)
    lane = iota((SEATS, count), 1)
    seat = iota((SEATS, count), 0)
    low = jnp.zeros((SEATS, count), I32)
    high = jnp.full((SEATS, count), count, I32)
    start = jnp.int32(0)
    dest_seat = iota((experts, 16, HEAD_DIM), 1) % SEATS
    dest = jnp.full((experts, 16, HEAD_DIM), -1, I32)
    for one in range(length_ref.shape[1]):
        stop = start + length_ref[0, one]
        low = jnp.where(seat == one, start, low)
        high = jnp.where(seat == one, stop, high)
        dest = jnp.where(dest_seat == one, target_ref[0, one] // slots, dest)
        start = stop
    allowed = (lane >= low) & (lane < high)
    contexts = []
    for head in range(head_width // HEAD_DIM):
        at = head * HEAD_DIM
        query = asked[head * SEATS : (head + 1) * SEATS]
        probs = softmax(dot_t(query, fresh_ref[:, at : at + HEAD_DIM]), allowed)
        at += head_width
        contexts.append(dot(probs, fresh_ref[:, at : at + HEAD_DIM]))
    context = jnp.concatenate(contexts, axis=0)
    goes = dest == iota(dest.shape, 0)
    out_ref[...] = jnp.where(goes, context[None], 0.0).astype(BF)


def cache_kernel(projected_ref, cache_ref, length_ref, out_ref, *, positions):
    count = projected_ref.shape[0]
    cells = cache_ref.shape[0]
    head_width = cache_ref.shape[1] // 2
    lengths = to_column(length_ref[...])
    cell = iota((count, cells), 1) - iota((count, cells), 0) * positions
    allowed = (cell >= 0) & (cell < lengths)
    for head in range(head_width // HEAD_DIM):
        at = head * HEAD_DIM
        query = projected_ref[:, at : at + HEAD_DIM]
        probs = softmax(dot_t(query, cache_ref[:, at : at + HEAD_DIM]), allowed)
        value = cache_ref[:, head_width + at : head_width + at + HEAD_DIM]
        out_ref[:, at : at + HEAD_DIM] = dot(probs, value).astype(BF)


def merge_kernel(seat_ref, back_ref, own_ref, out_ref):
    count, head_width = own_ref.shape
    cells = back_ref.shape[0] * back_ref.shape[1]
    back = back_ref[...].reshape(cells, HEAD_DIM)
    side = (iota((count, cells), 1) // SEATS) % 2
    wanted = seat_ref[...] == iota((count, cells), 0)
    hit = jnp.sum(jnp.where(wanted, 1.0, 0.0), axis=1, keepdims=True) > 0.0
    for head in range(head_width // HEAD_DIM):
        pick = jnp.where(wanted & (side == head), 1.0, 0.0).astype(BF)
        at = head * HEAD_DIM
        own = own_ref[:, at : at + HEAD_DIM].astype(F32)
        out_ref[:, at : at + HEAD_DIM] = jnp.where(hit, dot(pick, back), own).astype(BF)


def output_kernel(group_ref, *refs):
    parts = (len(refs) - 3) // 3
    contexts = refs[:parts]
    maps = refs[parts : 3 * parts]
    moe_ref, encoded_ref, out_ref = refs[3 * parts :]
    half = moe_ref.shape[1] // 2
    encoder = group_ref[0] == 0
    for side in range(2):
        for low in range(side * half, (side + 1) * half, 512):
            at = low - side * half
            total = moe_ref[:, low : low + 512].astype(F32)
            for step in range(parts):
                total += dot_t(contexts[step][...], maps[side * parts + step][at : at + 512, :])
            kept = encoded_ref[:, low : low + 512].astype(F32)
            out_ref[:, low : low + 512] = jnp.where(encoder, kept, total).astype(BF)


def gather_steps(block, parts, both_groups):
    groups = (0, 1) if both_groups else (1,)
    got = [block]
    for step in range(1, parts):
        pairs = [(g * parts + i, g * parts + (i + step) % parts) for g in groups for i in range(parts)]
        got.append(lax.ppermute(block, ("group", "mp"), pairs))
    return got


def relay(block, parts, turn):
    pairs = [(parts + i, parts + (i + turn) % parts) for i in range(parts)]
    got = [block]
    for _ in range(1, parts):
        got.append(lax.ppermute(got[-1], ("group", "mp"), pairs))
    return got


def shape(*dims):
    return jax.ShapeDtypeStruct(dims, BF)


def body(
    rows,
    route,
    gate_int,
    moe_gain,
    w_in,
    w_out,
    attn_gain,
    attn_weight,
    src_len,
    target,
    cache,
    cache_len,
):
    experts = lax.axis_size("expert")
    parts = lax.axis_size("mp")
    _, count, width = rows.shape
    piece = width // parts
    group_place = lax.axis_index("group").reshape(1)
    expert_place = lax.axis_index("expert")
    mp_place = lax.axis_index("mp").reshape(1)
    head_width = attn_weight.shape[3]
    positions = cache.shape[1]
    sources = src_len.shape[1]

    digits = jnp.stack([target[0] // count, target[0] % count])
    digits = jnp.pad(digits, ((0, 14), (0, 128 - sources)), constant_values=255).astype(BF)
    digits = lax.all_gather(digits, "expert", axis=0, tiled=True).reshape(experts, 16, 128)
    digits = digits[:, :2, :SEATS].astype(I32)
    local = jnp.where(digits[:, 0] == expert_place, digits[:, 1], -1)
    asked_local = local.reshape(1, experts * SEATS)
    seat_local = jnp.concatenate([local, local], axis=1).reshape(1, experts * 16)

    own_map = attn_weight[0][:, 1, :]
    upper = relay(own_map[: width // 2], parts, 1)
    lower = relay(own_map[width // 2 :], parts, parts - 1)
    maps = upper + [lower[(parts - step) % parts] for step in range(parts)]

    buffer, place = call(
        dispatch_kernel,
        [shape(experts, 4 * CAPACITY, width // 4), jax.ShapeDtypeStruct((2, count), I32)],
        [],
        [route[0].T, rows[0], moe_gain],
    )
    arrived = lax.all_to_all(buffer, "expert", split_axis=0, concat_axis=0, tiled=True)
    partial_rows = call(
        expert_kernel,
        shape(experts, parts, 16, piece // 2),
        [],
        [arrived, w_in[0, 0], w_out[0, 0]],
    )
    returned = lax.all_to_all(
        partial_rows.reshape(experts * parts, 16, piece // 2),
        ("expert", "mp"),
        split_axis=0,
        concat_axis=0,
        tiled=True,
    )
    moe_piece = call(
        combine_kernel, shape(count, piece), [mp_place], [place, gate_int[0].T, rows[0], returned]
    )
    moe_rows, encoded, projected, asked = call(
        project_kernel,
        [
            shape(count, width),
            shape(count, width),
            shape(count, 2 * head_width),
            shape(experts, 16, HEAD_DIM),
        ],
        [mp_place],
        [
            *gather_steps(moe_piece, parts, True),
            attn_gain,
            attn_weight[0].reshape(width, 2 * head_width),
            asked_local,
        ],
    )

    asked = lax.all_to_all(asked, "expert", split_axis=0, concat_axis=0, tiled=True)
    fresh = lax.ppermute(projected, "group", [(0, 1)])
    sent = call(
        functools.partial(source_kernel, slots=count),
        shape(experts, 16, HEAD_DIM),
        [src_len, target],
        [asked, fresh],
    )
    back = lax.all_to_all(sent, "expert", split_axis=0, concat_axis=0, tiled=True)
    own = call(
        functools.partial(cache_kernel, positions=positions),
        shape(count, head_width),
        [],
        [projected, cache.reshape(count * positions, 2 * head_width), cache_len.reshape(1, count)],
    )
    context = call(merge_kernel, shape(count, head_width), [], [seat_local, back, own])
    step_rows = call(
        output_kernel,
        shape(count, width),
        [group_place],
        [*gather_steps(context, parts, False), *maps, moe_rows, encoded],
    )
    return (moe_rows[None], step_rows[None])


def solution(mesh):
    return jax.shard_map(
        body,
        mesh=mesh,
        in_specs=(
            P("group", "expert", None),
            P("group", "expert", None),
            P("group", "expert", None),
            P("group", None),
            P("group", "expert", None, "mp"),
            P("group", "expert", "mp", None),
            P("group", None),
            P("group", None, None, "mp"),
            P("expert", None),
            P("expert", None),
            P("expert", None, None, "mp"),
            P("expert"),
        ),
        out_specs=(P("group", "expert", None), P("group", "expert", None)),
        check_vma=False,
    )
```

```python
import functools
import math

import jax
import jax.numpy as jnp
from jax import lax
from jax.experimental import pallas as pl
from jax.experimental.pallas import tpu as pltpu
from jax.sharding import PartitionSpec as P

HEAD_DIM = 128
CAPACITY = 8
SEATS = 8
FFN_LIMIT = 50
AHEAD = 3
BF = jnp.bfloat16
F32 = jnp.float32
I32 = jnp.int32
EPS = 1e-05
SCALE = 1.0 / math.sqrt(HEAD_DIM)


def iota(shape, dim):
    return lax.broadcasted_iota(I32, shape, dim)


def dot(a, b):
    return jnp.dot(a, b, preferred_element_type=F32)


def dot_t(a, b):
    return lax.dot_general(a, b, (((1,), (1,)), ((), ())), preferred_element_type=F32)


def call(kernel, outs, scalars, arrays, streamed=(), scratch=(), limit=40):
    smem = pl.BlockSpec(memory_space=pltpu.SMEM)
    vmem = pl.BlockSpec(memory_space=pltpu.VMEM)
    still = pl.BlockSpec(memory_space=pltpu.HBM)
    return pl.pallas_call(
        kernel,
        out_shape=outs,
        in_specs=[smem] * len(scalars) + [vmem] * len(arrays) + [still] * len(streamed),
        out_specs=jax.tree.map(lambda _: vmem, outs),
        scratch_shapes=list(scratch),
        compiler_params=pltpu.CompilerParams(vmem_limit_bytes=limit * 2**20),
    )(*scalars, *arrays, *streamed)


def to_column(row):
    n = row.shape[1]
    return jnp.sum(
        jnp.where(iota((n, n), 0) == iota((n, n), 1), row, jnp.zeros_like(row)),
        axis=1,
        keepdims=True,
    )


def stack_halves(value):
    half = value.shape[2] // 2
    return jnp.concatenate([value[:, :, :half], value[:, :, half:]], axis=1)


def dispatch_kernel(
    _, route_ref, rows_ref, gain_ref, out_ref, place_ref
):
    experts = out_ref.shape[0]
    count, width = rows_ref.shape
    route = route_ref[...]
    first, second = route[0:1], route[1:2]
    names = iota((experts, count), 0)
    hit0 = names == first
    hit1 = names == second
    one0 = jnp.where(hit0, 1.0, 0.0)
    one1 = jnp.where(hit1, 1.0, 0.0)
    before = jnp.where(iota((count, count), 0) < iota((count, count), 1), 1.0, 0.0).astype(BF)
    seen0 = dot(one0.astype(BF), before)
    seen1 = dot(one1.astype(BF), before) + jnp.sum(one0, axis=1, keepdims=True)
    place0 = first * CAPACITY + jnp.sum(one0 * seen0, axis=0, keepdims=True).astype(I32)
    place1 = second * CAPACITY + jnp.sum(one1 * seen1, axis=0, keepdims=True).astype(I32)
    place_ref[0:1, :] = place0
    place_ref[1:2, :] = place1
    slots = iota((experts * CAPACITY, count), 0)
    table = jnp.where((slots == place0) | (slots == place1), 1.0, 0.0).astype(BF)
    values = rows_ref[...].astype(F32)
    center = values - jnp.mean(values, axis=-1, keepdims=True)
    spread = jnp.mean(center * center, axis=-1, keepdims=True)
    normed = (center * lax.rsqrt(spread + EPS) * gain_ref[...]).astype(BF)
    span = out_ref.shape[2]
    for pair in range(width // (2 * span)):
        both = [
            dot(table, normed[:, (2 * pair + i) * span : (2 * pair + i + 1) * span]).reshape(
                experts, CAPACITY, span
            )
            for i in range(2)
        ]
        out_ref[:, pair * 16 : pair * 16 + 16, :] = jnp.concatenate(both, axis=1).astype(BF)


def expert_kernel(
    rows_ref, w_in_at, w_out_at, out_ref, w_in_ref, w_out_ref, in_sems, out_sems
):
    sources, _, span = rows_ref.shape
    width = w_in_ref.shape[0]
    parts = out_ref.shape[1]
    piece = width // parts
    steps = width // span
    copies = [
        pltpu.make_async_copy(
            w_in_at.at[pl.ds(step * span, span)],
            w_in_ref.at[pl.ds(step * span, span)],
            in_sems.at[step],
        )
        for step in range(steps)
    ] + [
        pltpu.make_async_copy(
            w_out_at.at[:, pl.ds(step * piece, piece)],
            w_out_ref.at[:, pl.ds(step * piece, piece)],
            out_sems.at[step],
        )
        for step in range(parts)
    ]
    for copy in copies[:AHEAD]:
        copy.start()

    def arrived(at):
        copies[at].wait()
        if at + AHEAD < len(copies):
            copies[at + AHEAD].start()

    total = None
    for pair in range(steps // 2):
        both = rows_ref[:, pair * 16 : pair * 16 + 16, :].astype(F32)
        for i in range(2):
            one = both[:, i * CAPACITY : (i + 1) * CAPACITY, :].reshape(sources * CAPACITY, span)
            at = 2 * pair + i
            arrived(at)
            term = dot(one.astype(BF), w_in_ref[at * span : (at + 1) * span, :])
            total = term if total is None else total + term
    hidden = jnp.maximum(total, 0.0).astype(BF)
    for part in range(parts):
        arrived(steps + part)
        done = dot(hidden, w_out_ref[:, part * piece : (part + 1) * piece])
        out_ref[:, part] = stack_halves(done.reshape(sources, CAPACITY, piece)).astype(BF)


def combine_kernel(mp_ref, place_ref, gate_ref, rows_ref, back_ref, out_ref):
    parts = rows_ref.shape[1] // out_ref.shape[1]
    count, piece = out_ref.shape
    cells = back_ref.shape[0] * back_ref.shape[1]
    half = back_ref.shape[2]
    place = place_ref[...]
    gate = gate_ref[...].astype(F32)
    gate0 = to_column(gate[0:1])
    gate1 = to_column(gate[1:2])
    whole = gate0 + gate1
    cell = iota((count, cells), 1)
    cell_slot = (cell // (parts * 16)) * CAPACITY + cell % CAPACITY
    cell_half = (cell // CAPACITY) % 2
    keys = [jnp.where(cell_half == side, cell_slot, -1) for side in range(2)]
    picks = []
    for which in range(2):
        wanted = to_column(place[which : which + 1])
        for side in range(2):
            picks.append(jnp.where(keys[side] == wanted, 1.0, 0.0).astype(BF))
    got = dot(jnp.concatenate(picks, axis=0), back_ref[...].reshape(cells, half))
    got = got.astype(BF).astype(F32)
    row0 = jnp.concatenate([got[0:count], got[count : 2 * count]], axis=1)
    row1 = jnp.concatenate([got[2 * count : 3 * count], got[3 * count :]], axis=1)
    at = pl.multiple_of(mp_ref[0] * piece, piece)
    base = rows_ref[:, pl.ds(at, piece)].astype(F32)
    out_ref[...] = (base + ((gate0 / whole) * row0 + (gate1 / whole) * row1)).astype(BF)


def project_kernel(
    mp_ref, one_ref, two_ref, three_ref, four_ref, gain_ref, maps_ref, local_ref,
    moe_ref, encoded_ref, projected_ref, asked_ref,
):
    refs = [one_ref, two_ref, three_ref, four_ref]
    parts = len(refs)
    count, piece = one_ref.shape
    width = parts * piece
    blocks = [ref[...].astype(F32) for ref in refs]
    mean = sum(jnp.sum(block, axis=1, keepdims=True) for block in blocks) / width
    centers = [block - mean for block in blocks]
    spread = sum(jnp.sum(c * c, axis=1, keepdims=True) for c in centers) / width
    scale = lax.rsqrt(spread + EPS)
    total = None
    for step in range(parts):
        place = lax.rem(mp_ref[0] + (parts - step), parts)
        at = pl.ds(pl.multiple_of(place * piece, piece), piece)
        moe_ref[:, at] = refs[step][...]
        encoded = (centers[step] * scale * gain_ref[:, at]).astype(BF)
        encoded_ref[:, at] = encoded
        term = dot(encoded, maps_ref[at, :])
        total = term if total is None else total + term
    projected = total.astype(BF)
    projected_ref[...] = projected
    experts = asked_ref.shape[0]
    head_width = projected.shape[1] // 2
    query = projected[:, :head_width]
    wanted = to_column(local_ref[...])
    freed = jnp.where(iota((wanted.shape[0], count), 1) == wanted, 1.0, 0.0).astype(BF)
    asked = dot(freed, query).reshape(experts, SEATS, head_width)
    asked_ref[...] = stack_halves(asked).astype(BF)


def softmax(scores, allowed):
    scores = jnp.where(allowed, scores * SCALE, -1e30)
    raised = jnp.where(
        allowed, jnp.exp(scores - jnp.max(scores, axis=1, keepdims=True)), 0.0
    )
    return (raised / jnp.sum(raised, axis=1, keepdims=True)).astype(BF)


def source_kernel(length_ref, target_ref, asked_ref, fresh_ref, out_ref, *, slots):
    experts = asked_ref.shape[0]
    count = fresh_ref.shape[0]
    head_width = fresh_ref.shape[1] // 2
    asked = jnp.sum(asked_ref[...].astype(F32), axis=0).astype(BF)
    lane = iota((SEATS, count), 1)
    seat = iota((SEATS, count), 0)
    low = jnp.zeros((SEATS, count), I32)
    high = jnp.full((SEATS, count), count, I32)
    start = jnp.int32(0)
    dest_seat = iota((experts, 16, HEAD_DIM), 1) % SEATS
    dest = jnp.full((experts, 16, HEAD_DIM), -1, I32)
    for one in range(length_ref.shape[1]):
        stop = start + length_ref[0, one]
        low = jnp.where(seat == one, start, low)
        high = jnp.where(seat == one, stop, high)
        dest = jnp.where(dest_seat == one, target_ref[0, one] // slots, dest)
        start = stop
    allowed = (lane >= low) & (lane < high)
    contexts = []
    for head in range(head_width // HEAD_DIM):
        at = head * HEAD_DIM
        query = asked[head * SEATS : (head + 1) * SEATS]
        probs = softmax(dot_t(query, fresh_ref[:, at : at + HEAD_DIM]), allowed)
        at += head_width
        contexts.append(dot(probs, fresh_ref[:, at : at + HEAD_DIM]))
    context = jnp.concatenate(contexts, axis=0)
    goes = dest == iota(dest.shape, 0)
    out_ref[...] = jnp.where(goes, context[None], 0.0).astype(BF)


def cache_kernel(projected_ref, cache_ref, length_ref, out_ref, *, positions):
    count = projected_ref.shape[0]
    cells = cache_ref.shape[0]
    head_width = cache_ref.shape[1] // 2
    lengths = to_column(length_ref[...])
    cell = iota((count, cells), 1) - iota((count, cells), 0) * positions
    allowed = (cell >= 0) & (cell < lengths)
    for head in range(head_width // HEAD_DIM):
        at = head * HEAD_DIM
        query = projected_ref[:, at : at + HEAD_DIM]
        probs = softmax(dot_t(query, cache_ref[:, at : at + HEAD_DIM]), allowed)
        value = cache_ref[:, head_width + at : head_width + at + HEAD_DIM]
        out_ref[:, at : at + HEAD_DIM] = dot(probs, value).astype(BF)


def merge_kernel(seat_ref, back_ref, own_ref, map_ref, out_ref):
    count, head_width = own_ref.shape
    cells = back_ref.shape[0] * back_ref.shape[1]
    back = back_ref[...].reshape(cells, HEAD_DIM)
    side = (iota((count, cells), 1) // SEATS) % 2
    wanted = seat_ref[...] == iota((count, cells), 0)
    hit = jnp.sum(jnp.where(wanted, 1.0, 0.0), axis=1, keepdims=True) > 0.0
    contexts = []
    for head in range(head_width // HEAD_DIM):
        pick = jnp.where(wanted & (side == head), 1.0, 0.0).astype(BF)
        own = own_ref[:, head * HEAD_DIM : (head + 1) * HEAD_DIM].astype(F32)
        contexts.append(jnp.where(hit, dot(pick, back), own).astype(BF))
    context = jnp.concatenate(contexts, axis=1)
    for low in range(0, out_ref.shape[1], 512):
        out_ref[:, low : low + 512] = dot_t(context, map_ref[low : low + 512, :]).astype(BF)


def output_kernel(group_ref, moe_ref, encoded_ref, mixed_ref, out_ref):
    encoder = group_ref[0] == 0
    for low in range(0, out_ref.shape[1], 512):
        total = moe_ref[:, low : low + 512].astype(F32)
        for part in range(mixed_ref.shape[0]):
            total += mixed_ref[part, :, low : low + 512].astype(F32)
        kept = encoded_ref[:, low : low + 512].astype(F32)
        out_ref[:, low : low + 512] = jnp.where(encoder, kept, total).astype(BF)


def gather_steps(block, parts, both_groups):
    groups = (0, 1) if both_groups else (1,)
    got = [block]
    for step in range(1, parts):
        pairs = [(g * parts + i, g * parts + (i + step) % parts) for g in groups for i in range(parts)]
        got.append(lax.ppermute(block, ("group", "mp"), pairs))
    return got


def shape(*dims):
    return jax.ShapeDtypeStruct(dims, BF)


def body(
    rows,
    route,
    gate_int,
    moe_gain,
    w_in,
    w_out,
    attn_gain,
    attn_weight,
    src_len,
    target,
    cache,
    cache_len,
):
    experts = lax.axis_size("expert")
    parts = lax.axis_size("mp")
    _, count, width = rows.shape
    piece = width // parts
    group_place = lax.axis_index("group").reshape(1)
    expert_place = lax.axis_index("expert")
    mp_place = lax.axis_index("mp").reshape(1)
    head_width = attn_weight.shape[3]
    positions = cache.shape[1]
    sources = src_len.shape[1]

    def exchange(block):
        padded = jnp.pad(block, ((0, 7), (0, 128 - sources)), constant_values=-1)
        padded = jnp.broadcast_to(padded, (experts, 8, 128))
        padded = lax.all_to_all(padded, "expert", split_axis=0, concat_axis=0, tiled=True)
        return padded[:, 0]

    known = lax.cond(
        group_place[0] == 0, exchange, lambda block: jnp.zeros((experts, 128), I32), target
    )
    buffer, place = call(
        dispatch_kernel,
        [shape(experts, 4 * CAPACITY, width // 4), jax.ShapeDtypeStruct((2, count), I32)],
        [],
        [known, route[0].T, rows[0], moe_gain],
    )
    known = lax.ppermute(known, ("group", "expert"), [(i, experts + i) for i in range(experts)])
    local = known[:, :SEATS] - expert_place * count
    local = jnp.where((local >= 0) & (local < count), local, -1)
    asked_local = local.reshape(1, experts * SEATS)
    seat_local = jnp.concatenate([local, local], axis=1).reshape(1, experts * 16)
    arrived = lax.all_to_all(buffer, "expert", split_axis=0, concat_axis=0, tiled=True)
    partial_rows = call(
        expert_kernel,
        shape(experts, parts, 16, piece // 2),
        [],
        [arrived],
        [w_in[0, 0], w_out[0, 0]],
        [
            pltpu.VMEM(w_in.shape[2:], BF),
            pltpu.VMEM(w_out.shape[2:], BF),
            pltpu.SemaphoreType.DMA((4,)),
            pltpu.SemaphoreType.DMA((parts,)),
        ],
        limit=FFN_LIMIT,
    )
    returned = lax.all_to_all(
        partial_rows.reshape(experts * parts, 16, piece // 2),
        ("expert", "mp"),
        split_axis=0,
        concat_axis=0,
        tiled=True,
    )
    moe_piece = call(
        combine_kernel, shape(count, piece), [mp_place], [place, gate_int[0].T, rows[0], returned]
    )
    moe_rows, encoded, projected, asked = call(
        project_kernel,
        [
            shape(count, width),
            shape(count, width),
            shape(count, 2 * head_width),
            shape(experts, 16, HEAD_DIM),
        ],
        [mp_place],
        [
            *gather_steps(moe_piece, parts, True),
            attn_gain,
            attn_weight[0].reshape(width, 2 * head_width),
            asked_local,
        ],
    )

    asked = lax.cond(
        group_place[0] == 1,
        lambda block: lax.all_to_all(block, "expert", split_axis=0, concat_axis=0, tiled=True),
        lambda block: block,
        asked,
    )
    fresh = lax.ppermute(projected, "group", [(0, 1)])
    sent = call(
        functools.partial(source_kernel, slots=count),
        shape(experts, 16, HEAD_DIM),
        [src_len, target],
        [asked, fresh],
    )
    back = lax.all_to_all(sent, "expert", split_axis=0, concat_axis=0, tiled=True)
    own = call(
        functools.partial(cache_kernel, positions=positions),
        shape(count, head_width),
        [],
        [projected, cache.reshape(count * positions, 2 * head_width), cache_len.reshape(1, count)],
    )
    mixed = call(
        merge_kernel, shape(count, width), [], [seat_local, back, own, attn_weight[0][:, 1, :]]
    )
    everyone = lax.cond(
        group_place[0] == 1,
        lambda block: lax.all_to_all(
            jnp.broadcast_to(block, (parts, count, width)), "mp", split_axis=0, concat_axis=0, tiled=True
        ),
        lambda block: jnp.zeros((parts, count, width), BF),
        mixed,
    )
    step_rows = call(
        output_kernel,
        shape(count, width),
        [group_place],
        [moe_rows, encoded, everyone],
    )
    return (moe_rows[None], step_rows[None])


def solution(mesh):
    return jax.shard_map(
        body,
        mesh=mesh,
        in_specs=(
            P("group", "expert", None),
            P("group", "expert", None),
            P("group", "expert", None),
            P("group", None),
            P("group", "expert", None, "mp"),
            P("group", "expert", "mp", None),
            P("group", None),
            P("group", None, None, "mp"),
            P("expert", None),
            P("expert", None),
            P("expert", None, None, "mp"),
            P("expert"),
        ),
        out_specs=(P("group", "expert", None), P("group", "expert", None)),
        check_vma=False,
    )
```

```python
import functools
import math

import jax
import jax.numpy as jnp
from jax import lax
from jax.experimental import pallas as pl
from jax.experimental.pallas import tpu as pltpu
from jax.sharding import PartitionSpec as P

HEAD_DIM = 128
CAPACITY = 8
SEATS = 8
EXPERTS = 32
FFN_LIMIT = 50
AHEAD = 3
BF = jnp.bfloat16
F32 = jnp.float32
I32 = jnp.int32
EPS = 1e-05
SCALE = 1.0 / math.sqrt(HEAD_DIM)


def iota(shape, dim):
    return lax.broadcasted_iota(I32, shape, dim)


def dot(a, b):
    return jnp.dot(a, b, preferred_element_type=F32)


def dot_t(a, b):
    return lax.dot_general(a, b, (((1,), (1,)), ((), ())), preferred_element_type=F32)


def call(kernel, outs, scalars, arrays, streamed=(), scratch=(), limit=16):
    smem = pl.BlockSpec(memory_space=pltpu.SMEM)
    vmem = pl.BlockSpec(memory_space=pltpu.VMEM)
    still = pl.BlockSpec(memory_space=pltpu.HBM)
    return pl.pallas_call(
        kernel,
        out_shape=outs,
        in_specs=[smem] * len(scalars) + [vmem] * len(arrays) + [still] * len(streamed),
        out_specs=jax.tree.map(lambda _: vmem, outs),
        scratch_shapes=list(scratch),
        compiler_params=pltpu.CompilerParams(vmem_limit_bytes=limit * 2**20),
    )(*scalars, *arrays, *streamed)


def to_column(row):
    n = row.shape[1]
    return jnp.sum(
        jnp.where(iota((n, n), 0) == iota((n, n), 1), row, jnp.zeros_like(row)),
        axis=1,
        keepdims=True,
    )


def stack_halves(value):
    half = value.shape[2] // 2
    return jnp.concatenate([value[:, :, :half], value[:, :, half:]], axis=1)


def seat_rows(route_ref, rows_ref, gain_ref, place_ref, experts):
    count = rows_ref.shape[0]
    route = route_ref[...]
    first, second = route[0:1], route[1:2]
    names = iota((experts, count), 0)
    one0 = jnp.where(names == first, 1.0, 0.0)
    one1 = jnp.where(names == second, 1.0, 0.0)
    before = jnp.where(iota((count, count), 0) < iota((count, count), 1), 1.0, 0.0).astype(BF)
    seen0 = dot(one0.astype(BF), before)
    seen1 = dot(one1.astype(BF), before) + jnp.sum(one0, axis=1, keepdims=True)
    place0 = first * CAPACITY + jnp.sum(one0 * seen0, axis=0, keepdims=True).astype(I32)
    place1 = second * CAPACITY + jnp.sum(one1 * seen1, axis=0, keepdims=True).astype(I32)
    place_ref[0:1, :] = place0
    place_ref[1:2, :] = place1
    slots = iota((experts * CAPACITY, count), 0)
    table = jnp.where((slots == place0) | (slots == place1), 1.0, 0.0).astype(BF)
    values = rows_ref[...].astype(F32)
    center = values - jnp.mean(values, axis=-1, keepdims=True)
    spread = jnp.mean(center * center, axis=-1, keepdims=True)
    return (center * lax.rsqrt(spread + EPS) * gain_ref[...]).astype(BF), table


def dispatch_kernel(target_ref, route_ref, rows_ref, gain_ref, out_ref, place_ref):
    experts, _, span = out_ref.shape
    normed, table = seat_rows(route_ref, rows_ref, gain_ref, place_ref, experts)
    runs = normed.shape[1] // (2 * span)
    for run in range(runs):
        seated = dot(table, normed[:, 2 * run * span : 2 * (run + 1) * span])
        seated = stack_halves(seated.reshape(experts, CAPACITY, 2 * span))
        out_ref[:, 16 * run : 16 * run + 16, :] = seated.astype(BF)
    own = to_column(target_ref[...])
    sources, count = own.shape[0], rows_ref.shape[0]
    lane, seat = iota((sources, span), 1), iota((sources, span), 0)
    digits = jnp.where(lane == seat, own // count, 0) + jnp.where(lane == seat + SEATS, own % count, 0)
    digits = jnp.sum(digits.astype(F32), axis=0, keepdims=True)
    lane = iota((1, span), 1)
    digits = jnp.where((lane >= sources) & (lane < SEATS), 255.0, digits)
    out_ref[:, 16 * runs :, :] = jnp.broadcast_to(digits[None], (experts, 16, span)).astype(BF)


def dispatch_piece_kernel(
    mp_ref, route_ref, rows_ref, gain_ref, out_ref, place_ref, normed_ref
):
    experts, _, half = out_ref.shape
    normed, table = seat_rows(route_ref, rows_ref, gain_ref, place_ref, experts)
    normed_ref[...] = normed
    at = pl.multiple_of(mp_ref[0] * (2 * half), 2 * half)
    seated = dot(table, normed_ref[:, pl.ds(at, 2 * half)])
    out_ref[...] = stack_halves(seated.reshape(experts, CAPACITY, 2 * half)).astype(BF)


def add_kernel(parts_ref, out_ref):
    out_ref[...] = sum(parts_ref[at].astype(F32) for at in range(parts_ref.shape[0])).astype(BF)


def expert_kernel(rows_ref, w_in_at, w_out_at, out_ref, *refs, pieces):
    digits_ref, w_in_ref, w_out_ref, in_sems, out_sems = refs if len(refs) > 4 else (None, *refs)
    width = w_in_ref.shape[0]
    steps, parts = in_sems.shape[0], out_sems.shape[0]
    step_rows, piece = width // steps, width // parts
    copies = [
        pltpu.make_async_copy(
            w_in_at.at[pl.ds(step * step_rows, step_rows)],
            w_in_ref.at[pl.ds(step * step_rows, step_rows)],
            in_sems.at[step],
        )
        for step in range(steps)
    ] + [
        pltpu.make_async_copy(
            w_out_at.at[:, pl.ds(step * piece, piece)],
            w_out_ref.at[:, pl.ds(step * piece, piece)],
            out_sems.at[step],
        )
        for step in range(parts)
    ]
    for copy in copies[:AHEAD]:
        copy.start()

    def arrived(at):
        copies[at].wait()
        if at + AHEAD < len(copies):
            copies[at + AHEAD].start()

    total = None
    runs = steps if pieces else (rows_ref.shape[1] - 16) // 16
    for run in range(runs):
        if run % (runs // steps) == 0:
            arrived(run // (runs // steps))
        both = rows_ref[run] if pieces else rows_ref[:, 16 * run : 16 * run + 16, :]
        both = both.astype(F32)
        both = jnp.concatenate([both[:, :CAPACITY], both[:, CAPACITY:]], axis=2)
        sources, _, span = both.shape
        one = both.reshape(sources * CAPACITY, span).astype(BF)
        term = dot(one, w_in_ref[run * span : (run + 1) * span, :])
        total = term if total is None else total + term
    if not pieces:
        digits_ref[...] = rows_ref[:, 16 * runs :, :].astype(F32)[:, 0].astype(I32)
    hidden = jnp.maximum(total, 0.0).astype(BF)
    for part in range(parts):
        arrived(steps + part)
        done = dot(hidden, w_out_ref[:, part * piece : (part + 1) * piece])
        done = stack_halves(done.reshape(sources, CAPACITY, piece)).astype(BF)
        if pieces:
            out_ref[part] = done
        else:
            out_ref[:, part] = done


def combine_kernel(mp_ref, place_ref, gate_ref, rows_ref, back_ref, out_ref, *blank_ref):
    for ref in blank_ref:
        ref[...] = jnp.zeros_like(ref)
    count, piece = out_ref.shape
    cells = back_ref.shape[0] * back_ref.shape[1]
    run = cells // EXPERTS
    half = back_ref.shape[2]
    place = place_ref[...]
    gate = gate_ref[...].astype(F32)
    gate0 = to_column(gate[0:1])
    gate1 = to_column(gate[1:2])
    whole = gate0 + gate1
    cell = iota((count, cells), 1)
    cell_slot = (cell // run) * CAPACITY + cell % CAPACITY
    cell_half = (cell // CAPACITY) % 2
    keys = [jnp.where(cell_half == side, cell_slot, -1) for side in range(2)]
    picks = []
    for which in range(2):
        wanted = to_column(place[which : which + 1])
        for side in range(2):
            picks.append(jnp.where(keys[side] == wanted, 1.0, 0.0).astype(BF))
    got = dot(jnp.concatenate(picks, axis=0), back_ref[...].reshape(cells, half))
    got = got.astype(BF).astype(F32)
    row0 = jnp.concatenate([got[0:count], got[count : 2 * count]], axis=1)
    row1 = jnp.concatenate([got[2 * count : 3 * count], got[3 * count :]], axis=1)
    at = pl.multiple_of(mp_ref[0] * piece, piece)
    base = rows_ref[:, pl.ds(at, piece)].astype(F32)
    out_ref[...] = (base + ((gate0 / whole) * row0 + (gate1 / whole) * row1)).astype(BF)


def project_kernel(
    mp_ref, one_ref, two_ref, three_ref, four_ref, gain_ref, maps_ref, local_ref,
    moe_ref, encoded_ref, projected_ref, asked_ref,
):
    refs = [one_ref, two_ref, three_ref, four_ref]
    parts = len(refs)
    count, piece = one_ref.shape
    width = parts * piece
    blocks = [ref[...].astype(F32) for ref in refs]
    mean = sum(jnp.sum(block, axis=1, keepdims=True) for block in blocks) / width
    centers = [block - mean for block in blocks]
    spread = sum(jnp.sum(c * c, axis=1, keepdims=True) for c in centers) / width
    scale = lax.rsqrt(spread + EPS)
    total = None
    for step in range(parts):
        place = lax.rem(mp_ref[0] + (parts - step), parts)
        at = pl.ds(pl.multiple_of(place * piece, piece), piece)
        moe_ref[:, at] = refs[step][...]
        encoded = (centers[step] * scale * gain_ref[:, at]).astype(BF)
        encoded_ref[:, at] = encoded
        term = dot(encoded, maps_ref[at, :])
        total = term if total is None else total + term
    projected = total.astype(BF)
    projected_ref[...] = projected
    experts = asked_ref.shape[0]
    head_width = projected.shape[1] // 2
    query = projected[:, :head_width]
    wanted = to_column(local_ref[...])
    freed = jnp.where(iota((wanted.shape[0], count), 1) == wanted, 1.0, 0.0).astype(BF)
    asked = dot(freed, query).reshape(experts, SEATS, head_width)
    asked_ref[...] = stack_halves(asked).astype(BF)


def softmax(scores, allowed):
    scores = jnp.where(allowed, scores * SCALE, -1e30)
    raised = jnp.where(
        allowed, jnp.exp(scores - jnp.max(scores, axis=1, keepdims=True)), 0.0
    )
    return (raised / jnp.sum(raised, axis=1, keepdims=True)).astype(BF)


def source_kernel(length_ref, target_ref, asked_ref, fresh_ref, out_ref, *, slots):
    experts = asked_ref.shape[0]
    count = fresh_ref.shape[0]
    head_width = fresh_ref.shape[1] // 2
    sources = length_ref.shape[1]
    seat, source = iota((SEATS, sources), 0), iota((SEATS, sources), 1)
    lengths = jnp.broadcast_to(length_ref[...], (SEATS, sources)).astype(F32)
    places = jnp.broadcast_to(target_ref[...] // slots, (SEATS, sources)).astype(F32)
    used = iota((SEATS, 1), 0) < sources
    starts = jnp.sum(jnp.where(source < seat, lengths, 0.0), axis=1, keepdims=True)
    stops = jnp.sum(jnp.where(source <= seat, lengths, 0.0), axis=1, keepdims=True)
    dest = jnp.sum(jnp.where(source == seat, places, 0.0), axis=1, keepdims=True)
    dest = jnp.where(used, dest, -1.0)
    row = iota((SEATS, count), 1).astype(F32)
    allowed = ((row >= starts) & (row < stops)) | (iota((SEATS, count), 0) >= sources)
    asked = jnp.sum(asked_ref[...].astype(F32), axis=0).astype(BF)
    contexts = []
    for head in range(head_width // HEAD_DIM):
        at = head * HEAD_DIM
        query = asked[head * SEATS : (head + 1) * SEATS]
        probs = softmax(dot_t(query, fresh_ref[:, at : at + HEAD_DIM]), allowed)
        at += head_width
        contexts.append(dot(probs, fresh_ref[:, at : at + HEAD_DIM]))
    context = jnp.concatenate(contexts, axis=0)
    dest = jnp.broadcast_to(jnp.concatenate([dest, dest], axis=0), context.shape)
    goes = dest[None] == iota(out_ref.shape, 0).astype(F32)
    out_ref[...] = jnp.where(goes, context[None], 0.0).astype(BF)


def cache_kernel(projected_ref, cache_ref, length_ref, out_ref, *, positions):
    count = projected_ref.shape[0]
    cells = cache_ref.shape[0]
    head_width = cache_ref.shape[1] // 2
    lengths = to_column(length_ref[...])
    cell = iota((count, cells), 1) - iota((count, cells), 0) * positions
    allowed = (cell >= 0) & (cell < lengths)
    for head in range(head_width // HEAD_DIM):
        at = head * HEAD_DIM
        query = projected_ref[:, at : at + HEAD_DIM]
        probs = softmax(dot_t(query, cache_ref[:, at : at + HEAD_DIM]), allowed)
        value = cache_ref[:, head_width + at : head_width + at + HEAD_DIM]
        out_ref[:, at : at + HEAD_DIM] = dot(probs, value).astype(BF)


def merge_kernel(seat_ref, back_ref, own_ref, map_ref, out_ref):
    count, head_width = own_ref.shape
    cells = back_ref.shape[0] * back_ref.shape[1]
    back = back_ref[...].reshape(cells, HEAD_DIM)
    side = (iota((count, cells), 1) // SEATS) % 2
    wanted = seat_ref[...] == iota((count, cells), 0)
    hit = jnp.sum(jnp.where(wanted, 1.0, 0.0), axis=1, keepdims=True) > 0.0
    contexts = []
    for head in range(head_width // HEAD_DIM):
        pick = jnp.where(wanted & (side == head), 1.0, 0.0).astype(BF)
        own = own_ref[:, head * HEAD_DIM : (head + 1) * HEAD_DIM].astype(F32)
        contexts.append(jnp.where(hit, dot(pick, back), own).astype(BF))
    context = jnp.concatenate(contexts, axis=1)
    for low in range(0, out_ref.shape[1], 512):
        out_ref[:, low : low + 512] = dot_t(context, map_ref[low : low + 512, :]).astype(BF)


def output_kernel(group_ref, moe_ref, encoded_ref, mixed_ref, out_ref):
    encoder = group_ref[0] == 0
    for low in range(0, out_ref.shape[1], 512):
        total = moe_ref[:, low : low + 512].astype(F32)
        for part in range(mixed_ref.shape[0]):
            total += mixed_ref[part, :, low : low + 512].astype(F32)
        kept = encoded_ref[:, low : low + 512].astype(F32)
        out_ref[:, low : low + 512] = jnp.where(encoder, kept, total).astype(BF)


def gather_steps(block, parts, both_groups):
    groups = (0, 1) if both_groups else (1,)
    got = [block]
    for step in range(1, parts):
        pairs = [(g * parts + i, g * parts + (i + step) % parts) for g in groups for i in range(parts)]
        got.append(lax.ppermute(block, ("group", "mp"), pairs))
    return got


def shape(*dims):
    return jax.ShapeDtypeStruct(dims, BF)


def body(
    rows,
    route,
    gate_int,
    moe_gain,
    w_in,
    w_out,
    attn_gain,
    attn_weight,
    src_len,
    target,
    cache,
    cache_len,
):
    experts = lax.axis_size("expert")
    parts = lax.axis_size("mp")
    _, count, width = rows.shape
    piece = width // parts
    group_place = lax.axis_index("group").reshape(1)
    expert_place = lax.axis_index("expert")
    mp_place = lax.axis_index("mp").reshape(1)
    head_width = attn_weight.shape[3]
    positions = cache.shape[1]
    sources = src_len.shape[1]

    def experts_of(arrived, out, pieces):
        return call(
            functools.partial(expert_kernel, pieces=pieces),
            out,
            [],
            [arrived],
            [w_in[0, 0], w_out[0, 0]],
            [
                pltpu.VMEM(w_in.shape[2:], BF),
                pltpu.VMEM(w_out.shape[2:], BF),
                pltpu.SemaphoreType.DMA((4,)),
                pltpu.SemaphoreType.DMA((parts,)),
            ],
            limit=FFN_LIMIT,
        )

    def exchange(block, axis):
        return lax.all_to_all(block, axis, split_axis=0, concat_axis=0, tiled=True)

    named = jax.ShapeDtypeStruct((2, count), I32)
    noted = jax.ShapeDtypeStruct((experts, 128), I32)
    half = piece // 2

    def decoder_layer(block):
        buffer, place = call(
            dispatch_kernel,
            [shape(experts, width // HEAD_DIM * CAPACITY + 16, HEAD_DIM), named],
            [],
            [block, route[0].T, rows[0], moe_gain],
        )
        partial_rows, known = experts_of(
            exchange(buffer, "expert"), [shape(experts, parts, 16, half), noted], False
        )
        returned = exchange(partial_rows.reshape(experts * parts, 16, half), ("expert", "mp"))
        moe_piece = call(
            combine_kernel,
            shape(count, piece),
            [mp_place],
            [place, gate_int[0].T, rows[0], returned],
        )
        return moe_piece, known

    def encoder_layer(block):
        buffer, place = call(
            dispatch_piece_kernel,
            [shape(experts, 16, half), named],
            [mp_place],
            [route[0].T, rows[0], moe_gain],
            scratch=[pltpu.VMEM((count, width), BF)],
        )
        arrived = exchange(buffer, "expert")
        arrived = exchange(jnp.broadcast_to(arrived, (parts, experts, 16, half)), "mp")
        partial_rows = experts_of(arrived, shape(parts, experts, 16, half), True)
        summed = call(add_kernel, shape(experts, 16, half), [], [exchange(partial_rows, "mp")])
        returned = exchange(summed, "expert")
        return tuple(
            call(
                combine_kernel,
                [shape(count, piece), noted],
                [mp_place],
                [place, gate_int[0].T, rows[0], returned],
            )
        )

    moe_piece, known = lax.cond(group_place[0] == 0, encoder_layer, decoder_layer, target)
    local = jnp.where(known[:, :SEATS] == expert_place, known[:, SEATS : 2 * SEATS], -1)
    asked_local = local.reshape(1, experts * SEATS)
    seat_local = jnp.concatenate([local, local], axis=1).reshape(1, experts * 16)
    moe_rows, encoded, projected, asked = call(
        project_kernel,
        [
            shape(count, width),
            shape(count, width),
            shape(count, 2 * head_width),
            shape(experts, 16, HEAD_DIM),
        ],
        [mp_place],
        [
            *gather_steps(moe_piece, parts, True),
            attn_gain,
            attn_weight[0].reshape(width, 2 * head_width),
            asked_local,
        ],
    )

    asked = lax.cond(
        group_place[0] == 1,
        lambda block: lax.all_to_all(block, "expert", split_axis=0, concat_axis=0, tiled=True),
        lambda block: block,
        asked,
    )
    asked, cache = lax.optimization_barrier((asked, cache))
    fresh = lax.ppermute(projected, "group", [(0, 1)])
    sent = call(
        functools.partial(source_kernel, slots=count),
        shape(experts, 16, HEAD_DIM),
        [],
        [src_len, target, asked, fresh],
    )
    back = lax.all_to_all(sent, "expert", split_axis=0, concat_axis=0, tiled=True)
    own = call(
        functools.partial(cache_kernel, positions=positions),
        shape(count, head_width),
        [],
        [projected, cache.reshape(count * positions, 2 * head_width), cache_len.reshape(1, count)],
    )
    mixed = call(
        merge_kernel, shape(count, width), [], [seat_local, back, own, attn_weight[0][:, 1, :]]
    )
    everyone = lax.cond(
        group_place[0] == 1,
        lambda block: lax.all_to_all(
            jnp.broadcast_to(block, (parts, count, width)), "mp", split_axis=0, concat_axis=0, tiled=True
        ),
        lambda block: jnp.zeros((parts, count, width), BF),
        mixed,
    )
    step_rows = call(
        output_kernel,
        shape(count, width),
        [group_place],
        [moe_rows, encoded, everyone],
    )
    return (moe_rows[None], step_rows[None])


def solution(mesh):
    return jax.shard_map(
        body,
        mesh=mesh,
        in_specs=(
            P("group", "expert", None),
            P("group", "expert", None),
            P("group", "expert", None),
            P("group", None),
            P("group", "expert", None, "mp"),
            P("group", "expert", "mp", None),
            P("group", None),
            P("group", None, None, "mp"),
            P("expert", None),
            P("expert", None),
            P("expert", None, None, "mp"),
            P("expert"),
        ),
        out_specs=(P("group", "expert", None), P("group", "expert", None)),
        check_vma=False,
    )
```

```python
import functools
import math

import jax
import jax.numpy as jnp
from jax import lax
from jax.experimental import pallas as pl
from jax.experimental.pallas import tpu as pltpu
from jax.sharding import PartitionSpec as P

HEAD_DIM = 128
CAPACITY = 8
SEATS = 8
EXPERTS = 32
FFN_LIMIT = 24
BF = jnp.bfloat16
F32 = jnp.float32
I32 = jnp.int32
EPS = 1e-05
SCALE = 1.0 / math.sqrt(HEAD_DIM)


def iota(shape, dim):
    return lax.broadcasted_iota(I32, shape, dim)


def dot(a, b):
    return jnp.dot(a, b, preferred_element_type=F32)


def dot_t(a, b):
    return lax.dot_general(a, b, (((1,), (1,)), ((), ())), preferred_element_type=F32)


def call(kernel, outs, scalars, arrays, streamed=(), scratch=(), limit=16, work=0):
    smem = pl.BlockSpec(memory_space=pltpu.SMEM)
    vmem = pl.BlockSpec(memory_space=pltpu.VMEM)
    still = pl.BlockSpec(memory_space=pltpu.HBM)
    return pl.pallas_call(
        kernel,
        out_shape=outs,
        in_specs=[smem] * len(scalars) + [vmem] * len(arrays) + [still] * len(streamed),
        out_specs=jax.tree.map(lambda _: vmem, outs),
        scratch_shapes=list(scratch),
        compiler_params=pltpu.CompilerParams(vmem_limit_bytes=limit * 2**20),
        cost_estimate=pl.CostEstimate(flops=work, bytes_accessed=work // 256, transcendentals=0)
        if work
        else None,
    )(*scalars, *arrays, *streamed)


def to_column(row):
    n = row.shape[1]
    return jnp.sum(
        jnp.where(iota((n, n), 0) == iota((n, n), 1), row, jnp.zeros_like(row)),
        axis=1,
        keepdims=True,
    )


def stack_halves(value):
    half = value.shape[2] // 2
    return jnp.concatenate([value[:, :, :half], value[:, :, half:]], axis=1)


def seat_rows(route_ref, rows_ref, gain_ref, place_ref, experts):
    count = rows_ref.shape[0]
    route = route_ref[...]
    first, second = route[0:1], route[1:2]
    names = iota((experts, count), 0)
    one0 = jnp.where(names == first, 1.0, 0.0)
    one1 = jnp.where(names == second, 1.0, 0.0)
    before = jnp.where(iota((count, count), 0) < iota((count, count), 1), 1.0, 0.0).astype(BF)
    seen0 = dot(one0.astype(BF), before)
    seen1 = dot(one1.astype(BF), before) + jnp.sum(one0, axis=1, keepdims=True)
    place0 = first * CAPACITY + jnp.sum(one0 * seen0, axis=0, keepdims=True).astype(I32)
    place1 = second * CAPACITY + jnp.sum(one1 * seen1, axis=0, keepdims=True).astype(I32)
    place_ref[0:1, :] = place0
    place_ref[1:2, :] = place1
    slots = iota((experts * CAPACITY, count), 0)
    table = jnp.where((slots == place0) | (slots == place1), 1.0, 0.0).astype(BF)
    values = rows_ref[...].astype(F32)
    center = values - jnp.mean(values, axis=-1, keepdims=True)
    spread = jnp.mean(center * center, axis=-1, keepdims=True)
    return (center * lax.rsqrt(spread + EPS) * gain_ref[...]).astype(BF), table


def dispatch_kernel(target_ref, route_ref, rows_ref, gain_ref, out_ref, place_ref):
    experts, _, span = out_ref.shape
    normed, table = seat_rows(route_ref, rows_ref, gain_ref, place_ref, experts)
    runs = normed.shape[1] // (2 * span)
    for run in range(runs):
        seated = dot(table, normed[:, 2 * run * span : 2 * (run + 1) * span])
        seated = stack_halves(seated.reshape(experts, CAPACITY, 2 * span))
        out_ref[:, 16 * run : 16 * run + 16, :] = seated.astype(BF)
    own = to_column(target_ref[...])
    sources, count = own.shape[0], rows_ref.shape[0]
    lane, seat = iota((sources, span), 1), iota((sources, span), 0)
    digits = jnp.where(lane == seat, own // count, 0) + jnp.where(lane == seat + SEATS, own % count, 0)
    digits = jnp.sum(digits.astype(F32), axis=0, keepdims=True)
    lane = iota((1, span), 1)
    digits = jnp.where((lane >= sources) & (lane < SEATS), 255.0, digits)
    out_ref[:, 16 * runs :, :] = jnp.broadcast_to(digits[None], (experts, 16, span)).astype(BF)


def dispatch_piece_kernel(
    mp_ref, route_ref, rows_ref, gain_ref, out_ref, place_ref, normed_ref
):
    experts, _, half = out_ref.shape
    normed, table = seat_rows(route_ref, rows_ref, gain_ref, place_ref, experts)
    normed_ref[...] = normed
    at = pl.multiple_of(mp_ref[0] * (2 * half), 2 * half)
    seated = dot(table, normed_ref[:, pl.ds(at, 2 * half)])
    out_ref[...] = stack_halves(seated.reshape(experts, CAPACITY, 2 * half)).astype(BF)


def add_kernel(parts_ref, out_ref):
    out_ref[...] = sum(parts_ref[at].astype(F32) for at in range(parts_ref.shape[0])).astype(BF)


def expert_kernel(rows_ref, w_in_ref, w_out_ref, out_ref, *digits_ref, pieces):
    width = w_in_ref.shape[0]
    parts = out_ref.shape[0] if pieces else out_ref.shape[1]
    piece = width // parts
    total = None
    runs = rows_ref.shape[0] if pieces else (rows_ref.shape[1] - 16) // 16
    for run in range(runs):
        both = rows_ref[run] if pieces else rows_ref[:, 16 * run : 16 * run + 16, :]
        both = both.astype(F32)
        both = jnp.concatenate([both[:, :CAPACITY], both[:, CAPACITY:]], axis=2)
        sources, _, span = both.shape
        one = both.reshape(sources * CAPACITY, span).astype(BF)
        term = dot(one, w_in_ref[run * span : (run + 1) * span, :])
        total = term if total is None else total + term
    if not pieces:
        digits_ref[0][...] = rows_ref[:, 16 * runs :, :].astype(F32)[:, 0].astype(I32)
    hidden = jnp.maximum(total, 0.0).astype(BF)
    for part in range(parts):
        done = dot(hidden, w_out_ref[:, part * piece : (part + 1) * piece])
        done = stack_halves(done.reshape(sources, CAPACITY, piece)).astype(BF)
        if pieces:
            out_ref[part] = done
        else:
            out_ref[:, part] = done


def combine_kernel(mp_ref, place_ref, gate_ref, rows_ref, back_ref, out_ref, *blank_ref):
    for ref in blank_ref:
        ref[...] = jnp.zeros_like(ref)
    count, piece = out_ref.shape
    cells = back_ref.shape[0] * back_ref.shape[1]
    run = cells // EXPERTS
    half = back_ref.shape[2]
    place = place_ref[...]
    gate = gate_ref[...].astype(F32)
    gate0 = to_column(gate[0:1])
    gate1 = to_column(gate[1:2])
    whole = gate0 + gate1
    cell = iota((count, cells), 1)
    cell_slot = (cell // run) * CAPACITY + cell % CAPACITY
    cell_half = (cell // CAPACITY) % 2
    keys = [jnp.where(cell_half == side, cell_slot, -1) for side in range(2)]
    picks = []
    for which in range(2):
        wanted = to_column(place[which : which + 1])
        for side in range(2):
            picks.append(jnp.where(keys[side] == wanted, 1.0, 0.0).astype(BF))
    got = dot(jnp.concatenate(picks, axis=0), back_ref[...].reshape(cells, half))
    got = got.astype(BF).astype(F32)
    row0 = jnp.concatenate([got[0:count], got[count : 2 * count]], axis=1)
    row1 = jnp.concatenate([got[2 * count : 3 * count], got[3 * count :]], axis=1)
    at = pl.multiple_of(mp_ref[0] * piece, piece)
    base = rows_ref[:, pl.ds(at, piece)].astype(F32)
    out_ref[...] = (base + ((gate0 / whole) * row0 + (gate1 / whole) * row1)).astype(BF)


def project_kernel(
    mp_ref, one_ref, two_ref, three_ref, four_ref, gain_ref, maps_ref, local_ref,
    moe_ref, encoded_ref, projected_ref, asked_ref,
):
    refs = [one_ref, two_ref, three_ref, four_ref]
    parts = len(refs)
    count, piece = one_ref.shape
    width = parts * piece
    blocks = [ref[...].astype(F32) for ref in refs]
    mean = sum(jnp.sum(block, axis=1, keepdims=True) for block in blocks) / width
    centers = [block - mean for block in blocks]
    spread = sum(jnp.sum(c * c, axis=1, keepdims=True) for c in centers) / width
    scale = lax.rsqrt(spread + EPS)
    total = None
    for step in range(parts):
        place = lax.rem(mp_ref[0] + (parts - step), parts)
        at = pl.ds(pl.multiple_of(place * piece, piece), piece)
        moe_ref[:, at] = refs[step][...]
        encoded = (centers[step] * scale * gain_ref[:, at]).astype(BF)
        encoded_ref[:, at] = encoded
        term = dot(encoded, maps_ref[at, :])
        total = term if total is None else total + term
    projected = total.astype(BF)
    projected_ref[...] = projected
    experts = asked_ref.shape[0]
    head_width = projected.shape[1] // 2
    query = projected[:, :head_width]
    wanted = to_column(local_ref[...])
    freed = jnp.where(iota((wanted.shape[0], count), 1) == wanted, 1.0, 0.0).astype(BF)
    asked = dot(freed, query).reshape(experts, SEATS, head_width)
    asked_ref[...] = stack_halves(asked).astype(BF)


def softmax(scores, allowed):
    scores = jnp.where(allowed, scores * SCALE, -1e30)
    raised = jnp.where(
        allowed, jnp.exp(scores - jnp.max(scores, axis=1, keepdims=True)), 0.0
    )
    return (raised / jnp.sum(raised, axis=1, keepdims=True)).astype(BF)


def source_kernel(length_ref, target_ref, asked_ref, fresh_ref, out_ref, *, slots):
    experts = asked_ref.shape[0]
    count = fresh_ref.shape[0]
    head_width = fresh_ref.shape[1] // 2
    sources = length_ref.shape[1]
    seat, source = iota((SEATS, sources), 0), iota((SEATS, sources), 1)
    lengths = jnp.broadcast_to(length_ref[...], (SEATS, sources)).astype(F32)
    places = jnp.broadcast_to(target_ref[...] // slots, (SEATS, sources)).astype(F32)
    used = iota((SEATS, 1), 0) < sources
    starts = jnp.sum(jnp.where(source < seat, lengths, 0.0), axis=1, keepdims=True)
    stops = jnp.sum(jnp.where(source <= seat, lengths, 0.0), axis=1, keepdims=True)
    dest = jnp.sum(jnp.where(source == seat, places, 0.0), axis=1, keepdims=True)
    dest = jnp.where(used, dest, -1.0)
    row = iota((SEATS, count), 1).astype(F32)
    allowed = ((row >= starts) & (row < stops)) | (iota((SEATS, count), 0) >= sources)
    asked = jnp.sum(asked_ref[...].astype(F32), axis=0).astype(BF)
    contexts = []
    for head in range(head_width // HEAD_DIM):
        at = head * HEAD_DIM
        query = asked[head * SEATS : (head + 1) * SEATS]
        probs = softmax(dot_t(query, fresh_ref[:, at : at + HEAD_DIM]), allowed)
        at += head_width
        contexts.append(dot(probs, fresh_ref[:, at : at + HEAD_DIM]))
    context = jnp.concatenate(contexts, axis=0)
    dest = jnp.broadcast_to(jnp.concatenate([dest, dest], axis=0), context.shape)
    goes = dest[None] == iota(out_ref.shape, 0).astype(F32)
    out_ref[...] = jnp.where(goes, context[None], 0.0).astype(BF)


def cache_kernel(projected_ref, cache_ref, length_ref, out_ref, *, positions):
    count = projected_ref.shape[0]
    cells = cache_ref.shape[0]
    head_width = cache_ref.shape[1] // 2
    lengths = to_column(length_ref[...])
    cell = iota((count, cells), 1) - iota((count, cells), 0) * positions
    allowed = (cell >= 0) & (cell < lengths)
    for head in range(head_width // HEAD_DIM):
        at = head * HEAD_DIM
        query = projected_ref[:, at : at + HEAD_DIM]
        probs = softmax(dot_t(query, cache_ref[:, at : at + HEAD_DIM]), allowed)
        value = cache_ref[:, head_width + at : head_width + at + HEAD_DIM]
        out_ref[:, at : at + HEAD_DIM] = dot(probs, value).astype(BF)


def merge_kernel(seat_ref, back_ref, own_ref, map_ref, out_ref):
    count, head_width = own_ref.shape
    cells = back_ref.shape[0] * back_ref.shape[1]
    back = back_ref[...].reshape(cells, HEAD_DIM)
    side = (iota((count, cells), 1) // SEATS) % 2
    wanted = seat_ref[...] == iota((count, cells), 0)
    hit = jnp.sum(jnp.where(wanted, 1.0, 0.0), axis=1, keepdims=True) > 0.0
    contexts = []
    for head in range(head_width // HEAD_DIM):
        pick = jnp.where(wanted & (side == head), 1.0, 0.0).astype(BF)
        own = own_ref[:, head * HEAD_DIM : (head + 1) * HEAD_DIM].astype(F32)
        contexts.append(jnp.where(hit, dot(pick, back), own).astype(BF))
    context = jnp.concatenate(contexts, axis=1)
    for low in range(0, out_ref.shape[1], 512):
        out_ref[:, low : low + 512] = dot_t(context, map_ref[low : low + 512, :]).astype(BF)


def output_kernel(group_ref, moe_ref, encoded_ref, mixed_ref, out_ref):
    encoder = group_ref[0] == 0
    for low in range(0, out_ref.shape[1], 512):
        total = moe_ref[:, low : low + 512].astype(F32)
        for part in range(mixed_ref.shape[0]):
            total += mixed_ref[part, :, low : low + 512].astype(F32)
        kept = encoded_ref[:, low : low + 512].astype(F32)
        out_ref[:, low : low + 512] = jnp.where(encoder, kept, total).astype(BF)


def gather_steps(block, parts, both_groups):
    groups = (0, 1) if both_groups else (1,)
    got = [block]
    for step in range(1, parts):
        pairs = [(g * parts + i, g * parts + (i + step) % parts) for g in groups for i in range(parts)]
        got.append(lax.ppermute(block, ("group", "mp"), pairs))
    return got


def shape(*dims):
    return jax.ShapeDtypeStruct(dims, BF)


def body(
    rows,
    route,
    gate_int,
    moe_gain,
    w_in,
    w_out,
    attn_gain,
    attn_weight,
    src_len,
    target,
    cache,
    cache_len,
):
    experts = lax.axis_size("expert")
    parts = lax.axis_size("mp")
    _, count, width = rows.shape
    piece = width // parts
    group_place = lax.axis_index("group").reshape(1)
    expert_place = lax.axis_index("expert")
    mp_place = lax.axis_index("mp").reshape(1)
    head_width = attn_weight.shape[3]
    positions = cache.shape[1]
    sources = src_len.shape[1]

    def experts_of(arrived, out, pieces):
        return call(
            functools.partial(expert_kernel, pieces=pieces),
            out,
            [],
            [arrived, w_in[0, 0], w_out[0, 0]],
            limit=FFN_LIMIT,
        )

    def exchange(block, axis):
        return lax.all_to_all(block, axis, split_axis=0, concat_axis=0, tiled=True)

    named = jax.ShapeDtypeStruct((2, count), I32)
    noted = jax.ShapeDtypeStruct((experts, 128), I32)
    half = piece // 2

    def decoder_layer(block):
        buffer, place = call(
            dispatch_kernel,
            [shape(experts, width // HEAD_DIM * CAPACITY + 16, HEAD_DIM), named],
            [],
            [block, route[0].T, rows[0], moe_gain],
            work=2**34,
        )
        partial_rows, known = experts_of(
            exchange(buffer, "expert"), [shape(experts, parts, 16, half), noted], False
        )
        returned = exchange(partial_rows.reshape(experts * parts, 16, half), ("expert", "mp"))
        moe_piece = call(
            combine_kernel,
            shape(count, piece),
            [mp_place],
            [place, gate_int[0].T, rows[0], returned],
        )
        return moe_piece, known

    def encoder_layer(block):
        buffer, place = call(
            dispatch_piece_kernel,
            [shape(experts, 16, half), named],
            [mp_place],
            [route[0].T, rows[0], moe_gain],
            scratch=[pltpu.VMEM((count, width), BF)],
            work=2**34,
        )
        arrived = exchange(buffer, "expert")
        arrived = exchange(jnp.broadcast_to(arrived, (parts, experts, 16, half)), "mp")
        partial_rows = experts_of(arrived, shape(parts, experts, 16, half), True)
        summed = call(add_kernel, shape(experts, 16, half), [], [exchange(partial_rows, "mp")])
        returned = exchange(summed, "expert")
        return tuple(
            call(
                combine_kernel,
                [shape(count, piece), noted],
                [mp_place],
                [place, gate_int[0].T, rows[0], returned],
            )
        )

    moe_piece, known = lax.cond(group_place[0] == 0, encoder_layer, decoder_layer, target)
    local = jnp.where(known[:, :SEATS] == expert_place, known[:, SEATS : 2 * SEATS], -1)
    asked_local = local.reshape(1, experts * SEATS)
    seat_local = jnp.concatenate([local, local], axis=1).reshape(1, experts * 16)
    moe_rows, encoded, projected, asked = call(
        project_kernel,
        [
            shape(count, width),
            shape(count, width),
            shape(count, 2 * head_width),
            shape(experts, 16, HEAD_DIM),
        ],
        [mp_place],
        [
            *gather_steps(moe_piece, parts, True),
            attn_gain,
            attn_weight[0].reshape(width, 2 * head_width),
            asked_local,
        ],
    )

    asked = lax.cond(
        group_place[0] == 1,
        lambda block: lax.all_to_all(block, "expert", split_axis=0, concat_axis=0, tiled=True),
        lambda block: block,
        asked,
    )
    asked, cache = lax.optimization_barrier((asked, cache))
    fresh = lax.ppermute(projected, "group", [(0, 1)])
    sent = call(
        functools.partial(source_kernel, slots=count),
        shape(experts, 16, HEAD_DIM),
        [],
        [src_len, target, asked, fresh],
    )
    back = lax.all_to_all(sent, "expert", split_axis=0, concat_axis=0, tiled=True)
    own = call(
        functools.partial(cache_kernel, positions=positions),
        shape(count, head_width),
        [],
        [projected, cache.reshape(count * positions, 2 * head_width), cache_len.reshape(1, count)],
    )
    mixed = call(
        merge_kernel, shape(count, width), [], [seat_local, back, own, attn_weight[0][:, 1, :]]
    )
    everyone = lax.cond(
        group_place[0] == 1,
        lambda block: lax.all_to_all(
            jnp.broadcast_to(block, (parts, count, width)), "mp", split_axis=0, concat_axis=0, tiled=True
        ),
        lambda block: jnp.zeros((parts, count, width), BF),
        mixed,
    )
    step_rows = call(
        output_kernel,
        shape(count, width),
        [group_place],
        [moe_rows, encoded, everyone],
    )
    return (moe_rows[None], step_rows[None])


def solution(mesh):
    return jax.shard_map(
        body,
        mesh=mesh,
        in_specs=(
            P("group", "expert", None),
            P("group", "expert", None),
            P("group", "expert", None),
            P("group", None),
            P("group", "expert", None, "mp"),
            P("group", "expert", "mp", None),
            P("group", None),
            P("group", None, None, "mp"),
            P("expert", None),
            P("expert", None),
            P("expert", None, None, "mp"),
            P("expert"),
        ),
        out_specs=(P("group", "expert", None), P("group", "expert", None)),
        check_vma=False,
    )
```

```python
import functools
import math

import jax
import jax.numpy as jnp
from jax import lax
from jax.experimental import pallas as pl
from jax.experimental.pallas import tpu as pltpu
from jax.sharding import PartitionSpec as P

HEAD_DIM = 128
CAPACITY = 8
SEATS = 8
EXPERTS = 32
FFN_LIMIT = 24
BF = jnp.bfloat16
F32 = jnp.float32
I32 = jnp.int32
EPS = 1e-05
SCALE = 1.0 / math.sqrt(HEAD_DIM)


def iota(shape, dim):
    return lax.broadcasted_iota(I32, shape, dim)


def dot(a, b):
    return jnp.dot(a, b, preferred_element_type=F32)


def dot_t(a, b):
    return lax.dot_general(a, b, (((1,), (1,)), ((), ())), preferred_element_type=F32)


def call(kernel, outs, scalars, arrays, streamed=(), scratch=(), limit=16, work=0):
    smem = pl.BlockSpec(memory_space=pltpu.SMEM)
    vmem = pl.BlockSpec(memory_space=pltpu.VMEM)
    still = pl.BlockSpec(memory_space=pltpu.HBM)
    return pl.pallas_call(
        kernel,
        out_shape=outs,
        in_specs=[smem] * len(scalars) + [vmem] * len(arrays) + [still] * len(streamed),
        out_specs=jax.tree.map(lambda _: vmem, outs),
        scratch_shapes=list(scratch),
        compiler_params=pltpu.CompilerParams(vmem_limit_bytes=limit * 2**20),
        cost_estimate=pl.CostEstimate(flops=work, bytes_accessed=work // 256, transcendentals=0)
        if work
        else None,
    )(*scalars, *arrays, *streamed)


def to_column(row):
    n = row.shape[1]
    return jnp.sum(
        jnp.where(iota((n, n), 0) == iota((n, n), 1), row, jnp.zeros_like(row)),
        axis=1,
        keepdims=True,
    )


def stack_halves(value):
    half = value.shape[2] // 2
    return jnp.concatenate([value[:, :, :half], value[:, :, half:]], axis=1)


def seat_rows(route_ref, rows_ref, gain_ref, place_ref, experts):
    count = rows_ref.shape[0]
    route = route_ref[...]
    first, second = route[0:1], route[1:2]
    names = iota((experts, count), 0)
    one0 = jnp.where(names == first, 1.0, 0.0)
    one1 = jnp.where(names == second, 1.0, 0.0)
    before = jnp.where(iota((count, count), 0) < iota((count, count), 1), 1.0, 0.0).astype(BF)
    seen0 = dot(one0.astype(BF), before)
    seen1 = dot(one1.astype(BF), before) + jnp.sum(one0, axis=1, keepdims=True)
    place0 = first * CAPACITY + jnp.sum(one0 * seen0, axis=0, keepdims=True).astype(I32)
    place1 = second * CAPACITY + jnp.sum(one1 * seen1, axis=0, keepdims=True).astype(I32)
    place_ref[0:1, :] = place0
    place_ref[1:2, :] = place1
    slots = iota((experts * CAPACITY, count), 0)
    table = jnp.where((slots == place0) | (slots == place1), 1.0, 0.0).astype(BF)
    values = rows_ref[...].astype(F32)
    center = values - jnp.mean(values, axis=-1, keepdims=True)
    spread = jnp.mean(center * center, axis=-1, keepdims=True)
    return (center * lax.rsqrt(spread + EPS) * gain_ref[...]).astype(BF), table


def dispatch_kernel(target_ref, route_ref, rows_ref, gain_ref, out_ref, place_ref):
    experts, _, span = out_ref.shape
    normed, table = seat_rows(route_ref, rows_ref, gain_ref, place_ref, experts)
    runs = normed.shape[1] // (2 * span)
    for run in range(runs):
        seated = dot(table, normed[:, 2 * run * span : 2 * (run + 1) * span])
        seated = stack_halves(seated.reshape(experts, CAPACITY, 2 * span))
        out_ref[:, 16 * run : 16 * run + 16, :] = seated.astype(BF)
    own = to_column(target_ref[...])
    sources, count = own.shape[0], rows_ref.shape[0]
    lane, seat = iota((sources, span), 1), iota((sources, span), 0)
    digits = jnp.where(lane == seat, own // count, 0) + jnp.where(lane == seat + SEATS, own % count, 0)
    digits = jnp.sum(digits.astype(F32), axis=0, keepdims=True)
    lane = iota((1, span), 1)
    digits = jnp.where((lane >= sources) & (lane < SEATS), 255.0, digits)
    out_ref[:, 16 * runs :, :] = jnp.broadcast_to(digits[None], (experts, 16, span)).astype(BF)


def dispatch_piece_kernel(
    mp_ref, route_ref, rows_ref, gain_ref, out_ref, place_ref, normed_ref
):
    experts, _, half = out_ref.shape
    normed, table = seat_rows(route_ref, rows_ref, gain_ref, place_ref, experts)
    normed_ref[...] = normed
    at = pl.multiple_of(mp_ref[0] * (2 * half), 2 * half)
    seated = dot(table, normed_ref[:, pl.ds(at, 2 * half)])
    out_ref[...] = stack_halves(seated.reshape(experts, CAPACITY, 2 * half)).astype(BF)


def add_kernel(parts_ref, out_ref):
    out_ref[...] = sum(parts_ref[at].astype(F32) for at in range(parts_ref.shape[0])).astype(BF)


def expert_kernel(rows_ref, w_in_ref, w_out_ref, out_ref, *digits_ref, pieces):
    width = w_in_ref.shape[0]
    parts = out_ref.shape[0] if pieces else out_ref.shape[1]
    piece = width // parts
    total = None
    runs = rows_ref.shape[0] if pieces else (rows_ref.shape[1] - 16) // 16
    for run in range(runs):
        both = rows_ref[run] if pieces else rows_ref[:, 16 * run : 16 * run + 16, :]
        both = both.astype(F32)
        both = jnp.concatenate([both[:, :CAPACITY], both[:, CAPACITY:]], axis=2)
        sources, _, span = both.shape
        one = both.reshape(sources * CAPACITY, span).astype(BF)
        term = dot(one, w_in_ref[run * span : (run + 1) * span, :])
        total = term if total is None else total + term
    if not pieces:
        digits_ref[0][...] = rows_ref[:, 16 * runs :, :].astype(F32)[:, 0].astype(I32)
    hidden = jnp.maximum(total, 0.0).astype(BF)
    for part in range(parts):
        done = dot(hidden, w_out_ref[:, part * piece : (part + 1) * piece])
        done = stack_halves(done.reshape(sources, CAPACITY, piece)).astype(BF)
        if pieces:
            out_ref[part] = done
        else:
            out_ref[:, part] = done


def combine_kernel(mp_ref, place_ref, gate_ref, rows_ref, back_ref, out_ref, *blank_ref):
    for ref in blank_ref:
        ref[...] = jnp.zeros_like(ref)
    count, piece = out_ref.shape
    cells = back_ref.shape[0] * back_ref.shape[1]
    run = cells // EXPERTS
    half = back_ref.shape[2]
    place = place_ref[...]
    gate = gate_ref[...].astype(F32)
    gate0 = to_column(gate[0:1])
    gate1 = to_column(gate[1:2])
    whole = gate0 + gate1
    cell = iota((count, cells), 1)
    cell_slot = (cell // run) * CAPACITY + cell % CAPACITY
    cell_half = (cell // CAPACITY) % 2
    keys = [jnp.where(cell_half == side, cell_slot, -1) for side in range(2)]
    picks = []
    for which in range(2):
        wanted = to_column(place[which : which + 1])
        for side in range(2):
            picks.append(jnp.where(keys[side] == wanted, 1.0, 0.0).astype(BF))
    got = dot(jnp.concatenate(picks, axis=0), back_ref[...].reshape(cells, half))
    got = got.astype(BF).astype(F32)
    row0 = jnp.concatenate([got[0:count], got[count : 2 * count]], axis=1)
    row1 = jnp.concatenate([got[2 * count : 3 * count], got[3 * count :]], axis=1)
    at = pl.multiple_of(mp_ref[0] * piece, piece)
    base = rows_ref[:, pl.ds(at, piece)].astype(F32)
    out_ref[...] = (base + ((gate0 / whole) * row0 + (gate1 / whole) * row1)).astype(BF)


def project_kernel(
    group_ref, mp_ref, one_ref, two_ref, three_ref, four_ref, gain_ref, maps_ref, local_ref,
    moe_ref, encoded_ref, projected_ref, asked_ref,
):
    refs = [one_ref, two_ref, three_ref, four_ref]
    parts = len(refs)
    count, piece = one_ref.shape
    width = parts * piece
    blocks = [ref[...].astype(F32) for ref in refs]
    mean = sum(jnp.sum(block, axis=1, keepdims=True) for block in blocks) / width
    centers = [block - mean for block in blocks]
    spread = sum(jnp.sum(c * c, axis=1, keepdims=True) for c in centers) / width
    scale = lax.rsqrt(spread + EPS)
    total = None
    for step in range(parts):
        place = lax.rem(mp_ref[0] + (parts - step), parts)
        at = pl.ds(pl.multiple_of(place * piece, piece), piece)
        moe_ref[:, at] = refs[step][...]
        encoded = (centers[step] * scale * gain_ref[:, at]).astype(BF)
        encoded_ref[:, at] = encoded
        term = dot(encoded, maps_ref[at, :])
        total = term if total is None else total + term
    projected = total.astype(BF)
    projected_ref[...] = projected
    experts = asked_ref.shape[0]
    head_width = projected.shape[1] // 2

    runs = count // 16
    tiles = 2 * head_width // HEAD_DIM
    packed = [
        total[:, tile * HEAD_DIM : (tile + 1) * HEAD_DIM].reshape(runs, 16, HEAD_DIM)
        for tile in range(tiles)
    ]
    packed.append(jnp.zeros((experts - runs * tiles, 16, HEAD_DIM), F32))
    wanted = to_column(local_ref[...])
    freed = jnp.where(iota((wanted.shape[0], count), 1) == wanted, 1.0, 0.0).astype(BF)
    asked = stack_halves(dot(freed, projected[:, :head_width]).reshape(experts, SEATS, head_width))
    asked_ref[...] = jnp.where(group_ref[0] == 0, jnp.concatenate(packed, axis=0), asked).astype(BF)


def softmax(scores, allowed):
    scores = jnp.where(allowed, scores * SCALE, -1e30)
    raised = jnp.where(
        allowed, jnp.exp(scores - jnp.max(scores, axis=1, keepdims=True)), 0.0
    )
    return (raised / jnp.sum(raised, axis=1, keepdims=True)).astype(BF)


def source_kernel(length_ref, target_ref, asked_ref, fresh_ref, out_ref, *, slots):
    heads = asked_ref.shape[1] // SEATS
    count = slots
    runs = count // 16
    sources = length_ref.shape[1]
    seat, source = iota((SEATS, sources), 0), iota((SEATS, sources), 1)
    lengths = jnp.broadcast_to(length_ref[...], (SEATS, sources)).astype(F32)
    places = jnp.broadcast_to(target_ref[...] // slots, (SEATS, sources)).astype(F32)
    used = iota((SEATS, 1), 0) < sources
    starts = jnp.sum(jnp.where(source < seat, lengths, 0.0), axis=1, keepdims=True)
    stops = jnp.sum(jnp.where(source <= seat, lengths, 0.0), axis=1, keepdims=True)
    dest = jnp.sum(jnp.where(source == seat, places, 0.0), axis=1, keepdims=True)
    dest = jnp.where(used, dest, -1.0)
    row = iota((SEATS, count), 1).astype(F32)
    allowed = ((row >= starts) & (row < stops)) | (iota((SEATS, count), 0) >= sources)
    asked = jnp.sum(asked_ref[...].astype(F32), axis=0).astype(BF)
    contexts = []
    for head in range(heads):
        query = asked[head * SEATS : (head + 1) * SEATS]
        keys, values = [
            fresh_ref[tile * runs : (tile + 1) * runs].reshape(count, HEAD_DIM)
            for tile in (head, heads + head)
        ]
        contexts.append(dot(softmax(dot_t(query, keys), allowed), values))
    context = jnp.concatenate(contexts, axis=0)
    dest = jnp.broadcast_to(jnp.concatenate([dest, dest], axis=0), context.shape)
    goes = dest[None] == iota(out_ref.shape, 0).astype(F32)
    out_ref[...] = jnp.where(goes, context[None], 0.0).astype(BF)


def cache_kernel(projected_ref, cache_ref, length_ref, out_ref, *, positions):
    count = projected_ref.shape[0]
    cells = cache_ref.shape[0]
    head_width = cache_ref.shape[1] // 2
    lengths = to_column(length_ref[...])
    cell = iota((count, cells), 1) - iota((count, cells), 0) * positions
    allowed = (cell >= 0) & (cell < lengths)
    for head in range(head_width // HEAD_DIM):
        at = head * HEAD_DIM
        query = projected_ref[:, at : at + HEAD_DIM]
        probs = softmax(dot_t(query, cache_ref[:, at : at + HEAD_DIM]), allowed)
        value = cache_ref[:, head_width + at : head_width + at + HEAD_DIM]
        out_ref[:, at : at + HEAD_DIM] = dot(probs, value).astype(BF)


def merge_kernel(seat_ref, back_ref, own_ref, map_ref, out_ref):
    count, head_width = own_ref.shape
    cells = back_ref.shape[0] * back_ref.shape[1]
    back = back_ref[...].reshape(cells, HEAD_DIM)
    side = (iota((count, cells), 1) // SEATS) % 2
    wanted = seat_ref[...] == iota((count, cells), 0)
    hit = jnp.sum(jnp.where(wanted, 1.0, 0.0), axis=1, keepdims=True) > 0.0
    contexts = []
    for head in range(head_width // HEAD_DIM):
        pick = jnp.where(wanted & (side == head), 1.0, 0.0).astype(BF)
        own = own_ref[:, head * HEAD_DIM : (head + 1) * HEAD_DIM].astype(F32)
        contexts.append(jnp.where(hit, dot(pick, back), own).astype(BF))
    context = jnp.concatenate(contexts, axis=1)
    for low in range(0, out_ref.shape[1], 512):
        out_ref[:, low : low + 512] = dot_t(context, map_ref[low : low + 512, :]).astype(BF)


def output_kernel(group_ref, moe_ref, encoded_ref, mixed_ref, out_ref):
    encoder = group_ref[0] == 0
    for low in range(0, out_ref.shape[1], 512):
        total = moe_ref[:, low : low + 512].astype(F32)
        for part in range(mixed_ref.shape[0]):
            total += mixed_ref[part, :, low : low + 512].astype(F32)
        kept = encoded_ref[:, low : low + 512].astype(F32)
        out_ref[:, low : low + 512] = jnp.where(encoder, kept, total).astype(BF)


def gather_steps(block, parts, both_groups):
    groups = (0, 1) if both_groups else (1,)
    got = [block]
    for step in range(1, parts):
        pairs = [(g * parts + i, g * parts + (i + step) % parts) for g in groups for i in range(parts)]
        got.append(lax.ppermute(block, ("group", "mp"), pairs))
    return got


def shape(*dims):
    return jax.ShapeDtypeStruct(dims, BF)


def body(
    rows,
    route,
    gate_int,
    moe_gain,
    w_in,
    w_out,
    attn_gain,
    attn_weight,
    src_len,
    target,
    cache,
    cache_len,
):
    experts = lax.axis_size("expert")
    parts = lax.axis_size("mp")
    _, count, width = rows.shape
    piece = width // parts
    group_place = lax.axis_index("group").reshape(1)
    expert_place = lax.axis_index("expert")
    mp_place = lax.axis_index("mp").reshape(1)
    head_width = attn_weight.shape[3]
    positions = cache.shape[1]
    sources = src_len.shape[1]

    def experts_of(arrived, out, pieces):
        return call(
            functools.partial(expert_kernel, pieces=pieces),
            out,
            [],
            [arrived, w_in[0, 0], w_out[0, 0]],
            limit=FFN_LIMIT,
        )

    def exchange(block, axis):
        return lax.all_to_all(block, axis, split_axis=0, concat_axis=0, tiled=True)

    named = jax.ShapeDtypeStruct((2, count), I32)
    noted = jax.ShapeDtypeStruct((experts, 128), I32)
    half = piece // 2

    def decoder_layer(block):
        buffer, place = call(
            dispatch_kernel,
            [shape(experts, width // HEAD_DIM * CAPACITY + 16, HEAD_DIM), named],
            [],
            [block, route[0].T, rows[0], moe_gain],
            work=2**34,
        )
        partial_rows, known = experts_of(
            exchange(buffer, "expert"), [shape(experts, parts, 16, half), noted], False
        )
        returned = exchange(partial_rows.reshape(experts * parts, 16, half), ("expert", "mp"))
        moe_piece = call(
            combine_kernel,
            shape(count, piece),
            [mp_place],
            [place, gate_int[0].T, rows[0], returned],
        )
        return moe_piece, known

    def encoder_layer(block):
        buffer, place = call(
            dispatch_piece_kernel,
            [shape(experts, 16, half), named],
            [mp_place],
            [route[0].T, rows[0], moe_gain],
            scratch=[pltpu.VMEM((count, width), BF)],
            work=2**34,
        )
        arrived = exchange(buffer, "expert")
        arrived = exchange(jnp.broadcast_to(arrived, (parts, experts, 16, half)), "mp")
        partial_rows = experts_of(arrived, shape(parts, experts, 16, half), True)
        summed = call(add_kernel, shape(experts, 16, half), [], [exchange(partial_rows, "mp")])
        returned = exchange(summed, "expert")
        return tuple(
            call(
                combine_kernel,
                [shape(count, piece), noted],
                [mp_place],
                [place, gate_int[0].T, rows[0], returned],
            )
        )

    moe_piece, known = lax.cond(group_place[0] == 0, encoder_layer, decoder_layer, target)
    local = jnp.where(known[:, :SEATS] == expert_place, known[:, SEATS : 2 * SEATS], -1)
    asked_local = local.reshape(1, experts * SEATS)
    seat_local = jnp.concatenate([local, local], axis=1).reshape(1, experts * 16)
    moe_rows, encoded, projected, asked = call(
        project_kernel,
        [
            shape(count, width),
            shape(count, width),
            shape(count, 2 * head_width),
            shape(experts, 16, HEAD_DIM),
        ],
        [group_place, mp_place],
        [
            *gather_steps(moe_piece, parts, True),
            attn_gain,
            attn_weight[0].reshape(width, 2 * head_width),
            asked_local,
        ],
    )

    asked = lax.cond(
        group_place[0] == 1,
        lambda block: lax.all_to_all(block, "expert", split_axis=0, concat_axis=0, tiled=True),
        lambda block: block,
        asked,
    )
    fresh = lax.ppermute(asked, "group", [(0, 1), (1, 0)])
    sent = call(
        functools.partial(source_kernel, slots=count),
        shape(experts, 16, HEAD_DIM),
        [],
        [src_len, target, asked, fresh],
    )
    sent, late_weight, cache = lax.optimization_barrier((sent, attn_weight, cache))
    back = lax.all_to_all(sent, "expert", split_axis=0, concat_axis=0, tiled=True)
    own = call(
        functools.partial(cache_kernel, positions=positions),
        shape(count, head_width),
        [],
        [projected, cache.reshape(count * positions, 2 * head_width), cache_len.reshape(1, count)],
    )
    mixed = call(
        merge_kernel, shape(count, width), [], [seat_local, back, own, late_weight[0][:, 1, :]]
    )
    everyone = lax.cond(
        group_place[0] == 1,
        lambda block: lax.all_to_all(
            jnp.broadcast_to(block, (parts, count, width)), "mp", split_axis=0, concat_axis=0, tiled=True
        ),
        lambda block: jnp.zeros((parts, count, width), BF),
        mixed,
    )
    step_rows = call(
        output_kernel,
        shape(count, width),
        [group_place],
        [moe_rows, encoded, everyone],
    )
    return (moe_rows[None], step_rows[None])


def solution(mesh):
    return jax.shard_map(
        body,
        mesh=mesh,
        in_specs=(
            P("group", "expert", None),
            P("group", "expert", None),
            P("group", "expert", None),
            P("group", None),
            P("group", "expert", None, "mp"),
            P("group", "expert", "mp", None),
            P("group", None),
            P("group", None, None, "mp"),
            P("expert", None),
            P("expert", None),
            P("expert", None, None, "mp"),
            P("expert"),
        ),
        out_specs=(P("group", "expert", None), P("group", "expert", None)),
        check_vma=False,
    )
```
